32 devices in a mesh: view: 8 (over z, y), brick: 4 (over x, core).
Axes of the slice: x: 2, y: 2, z: 4, core: 2. Of those that a mesh axis runs over, the one named last changes fastest.
Arguments:
- volume: float32 [8, 8, 32, 128], P('brick'), may hold values from -6 to 6
- offsets: float32 [8, 3], P('view'), may hold values from 0 to 1
- shifts: int32 [8, 2], P('view'), may hold values from 0 to 127
- order: int32 [8], P('view'), may hold values from 0 to 1
- cond: float32 [8, 8], P('view'), may hold values from -6 to 6
- w_in: float32 [16, 128], replicated, may hold values from -1.5 to 1.5
- w_mid: float32 [128, 128], replicated, may hold values from -0.5 to 0.5
- w_out: float32 [128, 4], replicated, may hold values from -0.5 to 0.5
- cot_image: float32 [8, 3, 32, 128], P('view', None, 'brick'), may hold values from -0.12 to 0.12
Outputs:
- image: float32 [8, 3, 32, 128], P('view', None, 'brick')
- grad_in: float32 [16, 128], replicated
- grad_mid: float32 [128, 128], replicated
- grad_out: float32 [128, 4], replicated
The draws below stay inside these ranges and needn't reach their ends.
Inputs may be any that keep to these rules, and one draw needn't show every extreme that they name: `order`: 0 marches towards higher slice numbers, 1 towards lower ones.
All inputs are finite; a program needn't handle non-finite values.
Results may differ from the reference program's by a relative error of at most 0.0003.
Values sent between devices are 32-bit elements; how exact they have to be, the bound alone decides.
A program may use at most 64 MiB of HBM per device.

```python
import jax
import jax.numpy as jnp
from jax import lax

PX = 32
PY = 128
CH = 8
COND = 8
HID = 128
FIN = 16
VIEWS = 8
NZ = 8


def touch_ends(values, own_key, low, top_value):
    place = [jax.random.randint(jax.random.fold_in(own_key, axis), (), 0, length) for axis, length in enumerate(values.shape)]
    widest = values.shape.index(max(values.shape))
    beside = place[:widest] + [(place[widest] + 1) % values.shape[widest]] + place[widest + 1:]
    return values.at[tuple(place)].set(low).at[tuple(beside)].set(top_value)


def levels(own_key, shape, cuts, least, high):
    loudness, own = 1.0, jax.random.fold_in(own_key, 6)
    for position, blocks in cuts:
        draws = jnp.exp(jax.random.uniform(jax.random.fold_in(own, position), (blocks,), jnp.float32, least / len(cuts), high / len(cuts)))
        loudness = loudness * jnp.repeat(draws, shape[position] // blocks).reshape([-1 if axis == position else 1 for axis in range(len(shape))])
    return loudness


def normal_values(stream_key, shape, scale, bound, cuts=(), kind=jnp.bfloat16):
    gain = levels(stream_key, shape, cuts, -0.22, 0.18) if cuts else 1.0
    entries = jax.random.normal(stream_key, shape, jnp.float32) * scale * gain
    return jnp.minimum(jnp.maximum(entries, -bound), bound).astype(kind)


def setup_inputs(seed: int = 0) -> dict:
    splits = jax.random.split(jax.random.key(seed), 10)
    volume = normal_values(splits[0], (NZ, CH, PX, PY), 1.0, 6.0, ((0, 4),), jnp.float32)
    offsets = jnp.clip(1.0 * jax.random.uniform(splits[1], (VIEWS, 3), jnp.float32) ** levels(splits[1], (VIEWS, 3), ((0, 8),), -0.2, 0.2), 0.0, 1.0)
    shifts = touch_ends(jax.random.randint(splits[2], (VIEWS, 2), 0, PY), jax.random.fold_in(splits[2], 1), 0, PY - 1).astype(jnp.int32)
    order = touch_ends(jax.random.randint(splits[3], (VIEWS,), 0, 2), jax.random.fold_in(splits[3], 1), 0, 1).astype(jnp.int32)
    cond = normal_values(splits[4], (VIEWS, COND), 1.0, 6.0, ((0, 8),), jnp.float32)
    w_in = normal_values(splits[5], (FIN, HID), FIN ** -0.5, 1.5, (), jnp.float32)
    w_mid = normal_values(splits[6], (HID, HID), HID ** -0.5, 0.5, (), jnp.float32)
    w_out = normal_values(splits[7], (HID, 4), HID ** -0.5, 0.5, (), jnp.float32)
    cot_image = normal_values(splits[8], (VIEWS, 3, PX, PY), 0.02, 0.12, ((0, 8), (2, 4)), jnp.float32)
    return dict(volume=volume, offsets=offsets, shifts=shifts, order=order, cond=cond, w_in=w_in, w_mid=w_mid, w_out=w_out, cot_image=cot_image)


STEP_DEPTH = 0.15
precise = lax.Precision.HIGHEST

def resample(padded, shift_view, fraction):
    depthwise = (1.0 - fraction[2]) * padded[:-1] + fraction[2] * padded[1:]
    shifted = jnp.roll(depthwise, -shift_view[0], 2)
    shifted = (1.0 - fraction[0]) * shifted + fraction[0] * jnp.roll(shifted, -1, 2)
    columns = jnp.roll(shifted, -shift_view[1], 3)
    return (1.0 - fraction[1]) * columns + fraction[1] * jnp.roll(columns, -1, 3)

def transfer(weights, density, condition):
    w_in, w_mid, w_out = weights
    spread = jnp.broadcast_to(condition[:, None], (condition.shape[0], density.shape[1]))
    features = jnp.concatenate([density, spread], 0)
    hidden = jax.nn.silu(jnp.einsum('io,in->on', w_in, features, precision=precise))
    hidden = jax.nn.silu(jnp.einsum('io,in->on', w_mid, hidden, precision=precise))
    result = jnp.einsum('io,in->on', w_out, hidden, precision=precise)
    return jnp.concatenate([jax.nn.softplus(result[:1]), jax.nn.sigmoid(result[1:])], 0)

def composite(emitted):
    optical = emitted[:, 0] * STEP_DEPTH
    optical_depth = jnp.cumsum(optical, 0)
    transmit = jnp.exp(optical - optical_depth)
    opacity = -jnp.expm1(-optical)
    colour = lax.optimization_barrier(jnp.sum((transmit * opacity)[:, None] * emitted[:, 1:], 0))
    return (colour, jnp.exp(-optical_depth[-1]))

def render(weights, volume, shift_view, fraction, facing, condition):
    padded = jnp.concatenate([volume, jnp.zeros_like(volume[:1])], 0)
    samples = resample(padded, shift_view, fraction)
    slices, channels, rows_all, cols_all = samples.shape
    flat = samples.transpose(1, 0, 2, 3).reshape(channels, slices * rows_all * cols_all)
    emitted = transfer(weights, flat, condition)
    emitted = emitted.reshape(4, slices, rows_all * cols_all).transpose(1, 0, 2)
    marching = jnp.where(facing == 1, emitted[::-1], emitted)
    colour, _ = composite(marching)
    return colour.reshape(3, rows_all, cols_all)

def reference(volume, offsets, shifts, order, cond, w_in, w_mid, w_out, cot_image):
    weights = (w_in, w_mid, w_out)

    def one_view(summed, element):
        fraction, shift_view, facing, condition, cotangent = element
        picture, pullback = jax.vjp(lambda params: render(params, volume, shift_view, fraction, facing, condition), weights)
        gradients = pullback(cotangent)[0]
        return (jax.tree.map(jnp.add, summed, gradients), picture)
    initial = jax.tree.map(jnp.zeros_like, weights)
    summed, pictures = lax.scan(one_view, initial, (offsets, shifts, order, cond, cot_image))
    return (pictures, summed[0], summed[1], summed[2])
```

```python
import functools

import jax
import jax.numpy as jnp
from jax import lax
from jax.experimental import pallas as pl
from jax.experimental.pallas import tpu as pltpu
from jax.sharding import PartitionSpec as P

STEP_DEPTH = 0.15
MESH = pl.DeviceIdType.MESH
F32 = jnp.float32
BF16 = jnp.bfloat16
TILE = 8


def split(x):
    high = x.astype(BF16)
    return high, (x - high.astype(F32)).astype(BF16)


def dot(a, b):
    return lax.dot_general(a, b, (((1,), (0,)), ((), ())), preferred_element_type=F32)


def blocks(a, b):
    out = lax.dot_general(a, b, (((1,), (1,)), ((), ())), preferred_element_type=F32)
    rows, cols = out.shape[0] // 2, out.shape[1] // 2
    return (out[rows:, cols:] + out[rows:, :cols] + out[:rows, cols:]) + out[:rows, :cols]


def activate(u):
    gate = 0.5 * jnp.tanh(0.5 * u) + 0.5
    h = u * gate
    return h, gate + h * (1.0 - gate)


def one_minus_exp(x):
    series = x * (1.0 - x * (1 / 2) * (1.0 - x * (1 / 3) * (1.0 - x * (1 / 4) * (1.0 - x * (1 / 5)))))
    e = jnp.exp(-x)
    return jnp.where(x < 0.0625, series, 1.0 - e), e


def kernel(
    views, bricks, S, R, C, RC, RB, hid,
    vol, offsets, shifts, order, cond, w_in, w_mid, w_out, cot,
    image, out_in, out_mid, out_out,
    halo, shifted, feats, h1, d1, h2, d2, emit, gate, part, cots,
    wi_s, wm_s, wo_s, wmb_s, wob_s, grads, landed, final,
    halo_sems, cot_send, cot_recv, part_send, part_recv, tile_send, tile_recv, last_send, last_recv,
):
    CH = 8
    N = views * bricks
    T = grads.shape[0]
    nch = R // RC
    n = RC * C
    v = lax.axis_index("view")
    b = lax.axis_index("brick")
    me = v * bricks + b

    def place(k):
        return (k // bricks, k % bricks)

    barrier = pltpu.get_barrier_semaphore()

    @pl.loop(1, N)
    def _(k):
        pl.semaphore_signal(barrier, inc=1, device_id=place((me + k) % N), device_id_type=MESH)

    f0, f1, f2 = offsets[0, 0], offsets[0, 1], offsets[0, 2]
    s0 = lax.rem(shifts[0, 0], R)
    s1 = lax.rem(shifts[0, 1], C)
    back = order[0] == 1

    for i in range(RB):
        cots[b * RB + i, pl.ds(0, 1), :] = jnp.zeros((1, C), F32)
        for c in range(3):
            cots[b * RB + i, pl.ds(1 + c, 1), :] = cot[0, c, pl.ds(i, 1), :]

    wi_hi, wi_lo = split(w_in[...].T)
    wi_s[...] = jnp.concatenate([wi_hi.astype(F32), wi_hi.astype(F32), wi_lo.astype(F32)], 1).astype(BF16)
    wm_hi, wm_lo = split(w_mid[...].T)
    wm_s[...] = jnp.concatenate([wm_hi, wm_hi, wm_lo], 1)
    wmb_hi, wmb_lo = split(w_mid[...])
    wmb_s[...] = jnp.concatenate([wmb_hi, wmb_hi, wmb_lo], 1)
    unit = (
        lax.broadcasted_iota(jnp.int32, (TILE, 4), 0) == lax.broadcasted_iota(jnp.int32, (TILE, 4), 1)
    ).astype(F32)
    wo_t = lax.dot_general(
        unit, w_out[...], (((1,), (1,)), ((), ())),
        preferred_element_type=F32, precision=lax.Precision.HIGHEST,
    )
    wo_hi = wo_t.astype(BF16).astype(F32)
    wo_lo = wo_t - wo_hi
    wo_s[...] = jnp.concatenate([wo_hi, wo_hi, wo_lo], 1).astype(BF16)
    wob_s[...] = jnp.concatenate([wo_hi, wo_hi, wo_lo, jnp.zeros_like(wo_lo)], 0).T.astype(BF16)

    def resample(s):
        for i in range(R):
            near = vol[s, pl.ds(i, CH, stride=R), :]
            far = vol[s + 1, pl.ds(i, CH, stride=R), :] if s + 1 < S else halo[pl.ds(i, CH, stride=R), :]
            deep = (1.0 - f2) * near + f2 * far
            first = pltpu.roll(deep, lax.rem(C - s1, C), 1)
            second = pltpu.roll(deep, lax.rem(2 * C - 1 - s1, C), 1)
            mixed = (1.0 - f1) * first + f1 * second
            shifted[s, i] = mixed
            shifted[s, R + i] = mixed
            if i == 0:
                shifted[s, 2 * R] = mixed

    row = lax.broadcasted_iota(jnp.int32, (CH, n), 0)
    cond_rows = jnp.zeros((CH, n), F32)
    for c in range(CH):
        cond_rows = jnp.where(row == c, cond[0, c], cond_rows)
    chan = lax.broadcasted_iota(jnp.int32, (RC, 4, C), 1)

    def forward(s, c):
        rows = shifted[s, pl.ds(s0 + c * RC, RC + 1)]
        mixed = (1.0 - f0) * rows[:-1] + f0 * rows[1:]
        feat = jnp.concatenate([jnp.concatenate([mixed[i] for i in range(RC)], 1), cond_rows], 0)
        hi, lo = split(feat)
        feats[s, c] = jnp.concatenate([hi, lo], 0)
        h, d = activate(dot(wi_s[...], jnp.concatenate([hi, lo, hi], 0)))
        d1[s, c] = d
        hi, lo = split(h)
        h1[s, c] = jnp.concatenate([hi, lo], 0)
        h, d = activate(dot(wm_s[...], jnp.concatenate([hi, lo, hi], 0)))
        d2[s, c] = d
        hi, lo = split(h)
        h2[s, c] = jnp.concatenate([hi, lo], 0)
        raw = dot(wo_s[...], jnp.concatenate([hi, lo, hi], 0))
        x = jnp.stack([raw[:4, i * C:(i + 1) * C] for i in range(RC)], 0)
        e = jnp.exp(-jnp.abs(x))
        r = 1.0 / (1.0 + e)
        sg = jnp.where(x >= 0, r, e * r)
        log1p = jnp.where(
            e < 0.0625, e * (1.0 - e * (1 / 2 - e * (1 / 3 - e * (1 / 4 - e * (1 / 5 - e * (1 / 6)))))), jnp.log(1.0 + e)
        )
        sp = jnp.maximum(x, 0.0) + log1p
        gate[s, pl.ds(c * RC, RC)] = sg
        emit[s, pl.ds(c * RC, RC)] = jnp.where(chan == 0, STEP_DEPTH * sp, sg)

    def marched(ref, rows, m):
        return jnp.where(back, ref[S - 1 - m, rows], ref[m, rows])

    def part_copy(c, k, brick):
        rows = pl.ds(c * RC, RC)
        return pltpu.make_async_remote_copy(
            src_ref=part.at[brick, rows], dst_ref=part.at[brick, rows],
            send_sem=part_send.at[c, k], recv_sem=part_recv.at[c, k],
            device_id=(v, (b + k) % bricks), device_id_type=MESH,
        )

    def composite(c):
        rows = pl.ds(c * RC, RC)
        transmit = jnp.ones((RC, 1, C), F32)
        colour = jnp.zeros((RC, 4, C), F32)
        for m in range(S):
            em = marched(emit, rows, m)
            opacity, e = one_minus_exp(em[:, 0:1, :])
            colour = colour + (transmit * opacity) * em
            transmit = transmit * e
        part[b, rows] = jnp.where(chan == 0, transmit, colour)

    def cot_copy(k, brick):
        rows = pl.ds(brick * RB, RB)
        return pltpu.make_async_remote_copy(
            src_ref=cots.at[rows], dst_ref=cots.at[rows],
            send_sem=cot_send.at[k], recv_sem=cot_recv.at[k],
            device_id=(v, (b + k) % bricks), device_id_type=MESH,
        )

    def halo_copy():
        return pltpu.make_async_remote_copy(
            src_ref=vol.at[0], dst_ref=halo, send_sem=halo_sems.at[0], recv_sem=halo_sems.at[1],
            device_id=(v, (b + bricks - 1) % bricks), device_id_type=MESH,
        )

    for s in range(S - 1):
        resample(s)

    pl.semaphore_wait(barrier, N - 1)

    @pl.when(b > 0)
    def _():
        halo_copy().start()

    for k in range(1, bricks):
        cot_copy(k, b).start()

    for s in range(S - 1):
        @pl.loop(0, nch)
        def _(c, s=s):
            forward(s, c)

    @pl.when(b == bricks - 1)
    def _():
        halo[...] = jnp.zeros_like(halo)

    @pl.when(b < bricks - 1)
    def _():
        halo_copy().wait_recv()

    resample(S - 1)

    @pl.loop(0, nch)
    def _(c):
        forward(S - 1, c)
        composite(c)
        for k in range(1, bricks):
            part_copy(c, k, b).start()

    for k in range(1, bricks):
        cot_copy(k, (b + bricks - k) % bricks).wait_recv()
    grads[...] = jnp.zeros_like(grads)
    position = jnp.where(back, bricks - 1 - b, b)

    def ordered(rows, p):
        return jnp.where(back, part[bricks - 1 - p, rows], part[p, rows])

    @pl.loop(0, nch)
    def _(c):
        rows = pl.ds(c * RC, RC)
        for k in range(1, bricks):
            part_copy(c, k, (b + bricks - k) % bricks).wait_recv()
        front = jnp.ones((RC, 1, C), F32)
        behind = jnp.zeros((RC, 4, C), F32)
        for p in range(bricks - 1):
            front = jnp.where(p < position, front * ordered(rows, p)[:, 0:1, :], front)
        for p in reversed(range(1, bricks)):
            here = ordered(rows, p)
            behind = jnp.where(p > position, here + here[:, 0:1, :] * behind, behind)
        grad = cots[rows] * front
        behind = jnp.sum(jnp.where(chan == 0, 0.0, grad * behind), 1, keepdims=True)
        transmit = jnp.ones((RC, 1, C), F32)
        steps = []
        for m in range(S):
            em = marched(emit, rows, m)
            opacity, e = one_minus_exp(em[:, 0:1, :])
            steps.append((em, marched(gate, rows, m), transmit * opacity, transmit * e))
            transmit = transmit * e
        tail = behind * transmit
        draws = [None] * S
        for m in reversed(range(S)):
            em, sg, weight, later = steps[m]
            q = jnp.sum(jnp.where(chan == 0, 0.0, grad * em), 1, keepdims=True)
            d_optical = q * later - tail
            tail = tail + q * weight
            draws[m] = jnp.where(chan == 0, d_optical * STEP_DEPTH * sg, grad * weight * (sg * (1.0 - sg)))
        for s in range(S):
            draw = jnp.where(back, draws[S - 1 - s], draws[s])
            draw = jnp.concatenate([draw[i] for i in range(RC)], 1)
            draw = jnp.concatenate([draw, jnp.zeros_like(draw)], 0)
            high = draw.astype(BF16).astype(F32)
            low = draw - high
            d_raw = jnp.concatenate([high, low, high, jnp.zeros_like(high)], 0).astype(BF16)
            g_out = blocks(d_raw[:2 * TILE], h2[s, c])
            du2 = dot(wob_s[...], d_raw) * d2[s, c]
            hi, lo = split(du2)
            g_mid = blocks(h1[s, c], jnp.concatenate([hi, lo], 0))
            du1 = dot(wmb_s[...], jnp.concatenate([hi, lo, hi], 0)) * d1[s, c]
            g_in = blocks(feats[s, c], jnp.concatenate(split(du1), 0))
            grads[0:2] += g_in.reshape(2, TILE, hid)
            grads[2:T - 1] += g_mid.reshape(T - 3, TILE, hid)
            grads[T - 1] += g_out

    def owner(t):
        return (t * N) // T

    def tile_copy(t, slot):
        return pltpu.make_async_remote_copy(
            src_ref=grads.at[t], dst_ref=landed.at[slot],
            send_sem=tile_send.at[t], recv_sem=tile_recv.at[slot],
            device_id=place(owner(t)), device_id_type=MESH,
        )

    def last_copy(t, k):
        return pltpu.make_async_remote_copy(
            src_ref=final.at[t], dst_ref=final.at[t],
            send_sem=last_send.at[k], recv_sem=last_recv.at[t],
            device_id=place((me + k) % N), device_id_type=MESH,
        )

    @pl.loop(0, T)
    def _(t):
        @pl.when(owner(t) != me)
        def _():
            tile_copy(t, (me - owner(t) + N - 1) % N).start()

    own = pl.ds(b * RB, RB)
    transmit = jnp.ones((RB, 1, C), F32)
    colour = jnp.zeros((RB, 4, C), F32)
    for p in range(bricks):
        here = ordered(own, p)
        colour = colour + transmit * here
        transmit = transmit * here[:, 0:1, :]
    for i in range(RB):
        for c in range(3):
            image[0, c, pl.ds(i, 1), :] = colour[i, 1 + c:2 + c, :]

    my_tile = (me * T + N - 1) // N
    owns = owner(my_tile) == me

    @pl.when(owns)
    def _():
        @pl.loop(0, N - 1)
        def _(k):
            tile_copy(my_tile, k).wait_recv()

        final[my_tile] = grads[my_tile] + jnp.sum(landed[...], 0)

        @pl.loop(1, N)
        def _(k):
            last_copy(my_tile, k).start()

    @pl.when(b > 0)
    def _():
        halo_copy().wait_send()

    for k in range(1, bricks):
        cot_copy(k, b).wait_send()

    @pl.loop(0, nch)
    def _(c):
        for k in range(1, bricks):
            part_copy(c, k, b).wait_send()

    @pl.loop(0, T)
    def _(t):
        @pl.when(owner(t) != me)
        def _():
            tile_copy(t, 0).wait_send()
            last_copy(t, 1).wait_recv()

    out_in[...] = final[0:2].reshape(2 * TILE, hid)
    out_mid[...] = final[2:T - 1].reshape(hid, hid)
    out_out[...] = final[T - 1][:4]

    @pl.when(owns)
    def _():
        @pl.loop(1, N)
        def _(k):
            last_copy(my_tile, k).wait_send()


def per_device(volume, offsets, shifts, order, cond, w_in, w_mid, w_out, cot_image):
    views, bricks = lax.axis_size("view"), lax.axis_size("brick")
    N = views * bricks
    S, CH, R, C = volume.shape
    RB = cot_image.shape[2]
    fin, hid = w_in.shape
    RC = min(8, R)
    nch = R // RC
    n = RC * C
    T = (fin + hid) // TILE + 1
    vmem = pl.BlockSpec(memory_space=pltpu.VMEM)
    smem = pl.BlockSpec(memory_space=pltpu.SMEM)
    kept = lambda rows, kind: pltpu.VMEM((S, nch, rows, n), kind)
    dma = lambda *shape: pltpu.SemaphoreType.DMA(shape)
    image, g_in, g_mid, g_out = pl.pallas_call(
        functools.partial(kernel, views, bricks, S, R, C, RC, RB, hid),
        out_shape=(
            jax.ShapeDtypeStruct((1, 3, RB, C), F32),
            jax.ShapeDtypeStruct((fin, hid), F32),
            jax.ShapeDtypeStruct((hid, hid), F32),
            jax.ShapeDtypeStruct((4, hid), F32),
        ),
        in_specs=[vmem, smem, smem, smem, smem, vmem, vmem, vmem, vmem],
        out_specs=(vmem, vmem, vmem, vmem),
        scratch_shapes=[
            pltpu.VMEM((CH * R, C), F32),
            pltpu.VMEM((S, 2 * R + 1, CH, C), F32),
            kept(2 * fin, BF16), kept(2 * hid, BF16), kept(hid, F32), kept(2 * hid, BF16), kept(hid, F32),
            pltpu.VMEM((S, R, 4, C), F32),
            pltpu.VMEM((S, R, 4, C), F32),
            pltpu.VMEM((bricks, R, 4, C), F32),
            pltpu.VMEM((R, 4, C), F32),
            pltpu.VMEM((hid, 3 * fin), BF16),
            pltpu.VMEM((hid, 3 * hid), BF16),
            pltpu.VMEM((TILE, 3 * hid), BF16),
            pltpu.VMEM((hid, 3 * hid), BF16),
            pltpu.VMEM((hid, 4 * TILE), BF16),
            pltpu.VMEM((T, TILE, hid), F32),
            pltpu.VMEM((N - 1, TILE, hid), F32),
            pltpu.VMEM((T, TILE, hid), F32),
            dma(2), dma(bricks), dma(bricks), dma(nch, bricks), dma(nch, bricks),
            dma(T), dma(N - 1), dma(N), dma(T),
        ],
        compiler_params=pltpu.CompilerParams(
            collective_id=0, has_side_effects=True, vmem_limit_bytes=56 * 1024 * 1024
        ),
        cost_estimate=pl.CostEstimate(
            flops=2 * S * R * C * hid * (3 * hid + 3 * fin + 12), bytes_accessed=4 * volume.size,
            transcendentals=2 * S * R * C * hid,
        ),
    )(volume.reshape(S, CH * R, C), offsets, shifts, order, cond, w_in, w_mid, w_out, cot_image)
    return image, g_in, g_mid, g_out.T


def solution(mesh):
    placed = (
        P("brick", None, None, None),
        P("view", None),
        P("view", None),
        P("view"),
        P("view", None),
        P(),
        P(),
        P(),
        P("view", None, "brick", None),
    )
    return jax.shard_map(
        per_device,
        mesh=mesh,
        in_specs=placed,
        out_specs=(P("view", None, "brick", None), P(), P(), P()),
        check_vma=False,
    )
```

```python
import functools

import jax
import jax.numpy as jnp
from jax import lax
from jax.experimental import pallas as pl
from jax.experimental.pallas import tpu as pltpu
from jax.sharding import PartitionSpec as P

STEP_DEPTH = 0.15
MESH = pl.DeviceIdType.MESH
F32 = jnp.float32
BF16 = jnp.bfloat16
TILE = 8


def split(x):
    high = x.astype(BF16)
    return high, (x - high.astype(F32)).astype(BF16)


def dot(a, b):
    return lax.dot_general(a, b, (((1,), (0,)), ((), ())), preferred_element_type=F32)


def stacked(high, low):
    return jnp.concatenate([jnp.concatenate([high, high], 1), jnp.concatenate([low, low], 1)], 0)


def dot_stacked(a, b):
    out = dot(a, b)
    rows = out.shape[0] // 2
    return out[:rows] + out[rows:]


def blocks(a, b):
    out = lax.dot_general(a, b, (((1,), (1,)), ((), ())), preferred_element_type=F32)
    rows, cols = out.shape[0] // 2, out.shape[1] // 2
    return (out[rows:, cols:] + out[rows:, :cols] + out[:rows, cols:]) + out[:rows, :cols]


def activate(u):
    gate = 0.5 * jnp.tanh(0.5 * u) + 0.5
    h = u * gate
    return h, gate + h * (1.0 - gate)


def one_minus_exp(x):
    series = x * (1.0 - x * (1 / 2) * (1.0 - x * (1 / 3) * (1.0 - x * (1 / 4) * (1.0 - x * (1 / 5)))))
    e = jnp.exp(-x)
    return jnp.where(x < 0.0625, series, 1.0 - e), e


def kernel(
    views, bricks, S, R, C, RC, RB, hid,
    vol, offsets, shifts, order, cond, w_in, w_mid, w_out, cot,
    image, final_out,
    halo, shifted, feats, h1, d1, h2, d2, emit, gate, part, cots,
    wi_s, wm_s, wo_s, wmb_s, wob_s, grads, landed, final,
    halo_sems, cot_send, cot_recv, part_send, part_recv, tile_send, tile_recv, last_send, last_recv,
):
    CH = 8
    N = views * bricks
    T = grads.shape[0]
    nch = R // RC
    n = RC * C
    v = lax.axis_index("view")
    b = lax.axis_index("brick")
    me = v * bricks + b

    def place(k):
        return (k // bricks, k % bricks)

    barrier = pltpu.get_barrier_semaphore()

    @pl.loop(1, N)
    def _(k):
        pl.semaphore_signal(barrier, inc=1, device_id=place((me + k) % N), device_id_type=MESH)

    f0, f1, f2 = offsets[0, 0], offsets[0, 1], offsets[0, 2]
    s0 = lax.rem(shifts[0, 0], R)
    s1 = lax.rem(shifts[0, 1], C)
    back = order[0] == 1

    for i in range(RB):
        cots[b * RB + i, pl.ds(0, 1), :] = jnp.zeros((1, C), F32)
        for c in range(3):
            cots[b * RB + i, pl.ds(1 + c, 1), :] = cot[0, c, pl.ds(i, 1), :]

    wi_hi, wi_lo = split(w_in[...].T)
    wi_s[...] = jnp.concatenate([wi_hi.astype(F32), wi_hi.astype(F32), wi_lo.astype(F32)], 1).astype(BF16)
    wm_hi, wm_lo = split(w_mid[...].T)
    wm_s[...] = stacked(wm_hi, wm_lo)
    wmb_hi, wmb_lo = split(w_mid[...])
    wmb_s[...] = stacked(wmb_hi, wmb_lo)
    wo_t = jnp.concatenate([w_out[...], jnp.zeros_like(w_out)], 0)
    wo_hi = wo_t.astype(BF16).astype(F32)
    wo_lo = wo_t - wo_hi
    wo_s[...] = stacked(wo_hi, wo_lo).astype(BF16)
    wob_s[...] = jnp.concatenate([wo_hi, wo_hi, wo_lo, jnp.zeros_like(wo_lo)], 0).T.astype(BF16)

    def resample(s):
        for i in range(R):
            near = vol[s, pl.ds(i, CH, stride=R), :]
            far = vol[s + 1, pl.ds(i, CH, stride=R), :] if s + 1 < S else halo[pl.ds(i, CH, stride=R), :]
            deep = (1.0 - f2) * near + f2 * far
            first = pltpu.roll(deep, lax.rem(C - s1, C), 1)
            second = pltpu.roll(deep, lax.rem(2 * C - 1 - s1, C), 1)
            mixed = (1.0 - f1) * first + f1 * second
            shifted[s, i] = mixed
            shifted[s, R + i] = mixed
            if i == 0:
                shifted[s, 2 * R] = mixed

    row = lax.broadcasted_iota(jnp.int32, (CH, n), 0)
    cond_rows = jnp.zeros((CH, n), F32)
    for c in range(CH):
        cond_rows = jnp.where(row == c, cond[0, c], cond_rows)
    chan = lax.broadcasted_iota(jnp.int32, (RC, 4, C), 1)

    def forward(s, c):
        rows = shifted[s, pl.ds(s0 + c * RC, RC + 1)]
        mixed = (1.0 - f0) * rows[:-1] + f0 * rows[1:]
        feat = jnp.concatenate([jnp.concatenate([mixed[i] for i in range(RC)], 1), cond_rows], 0)
        hi, lo = split(feat)
        feats[s, c] = jnp.concatenate([hi, lo], 0)
        h, d = activate(dot(wi_s[...], jnp.concatenate([hi, lo, hi], 0)))
        d1[s, c] = d
        both = jnp.concatenate(split(h), 0)
        h1[s, c] = both
        h, d = activate(dot_stacked(wm_s[...], both))
        d2[s, c] = d
        both = jnp.concatenate(split(h), 0)
        h2[s, c] = both
        raw = dot_stacked(wo_s[...], both)
        x = jnp.stack([raw[:4, i * C:(i + 1) * C] for i in range(RC)], 0)
        e = jnp.exp(-jnp.abs(x))
        r = 1.0 / (1.0 + e)
        sg = jnp.where(x >= 0, r, e * r)
        log1p = jnp.where(
            e < 0.0625, e * (1.0 - e * (1 / 2 - e * (1 / 3 - e * (1 / 4 - e * (1 / 5 - e * (1 / 6)))))), jnp.log(1.0 + e)
        )
        sp = jnp.maximum(x, 0.0) + log1p
        gate[s, pl.ds(c * RC, RC)] = sg
        emit[s, pl.ds(c * RC, RC)] = jnp.where(chan == 0, STEP_DEPTH * sp, sg)

    def marched(ref, rows, m):
        return jnp.where(back, ref[S - 1 - m, rows], ref[m, rows])

    def part_copy(c, k, brick):
        rows = pl.ds(c * RC, RC)
        return pltpu.make_async_remote_copy(
            src_ref=part.at[brick, rows], dst_ref=part.at[brick, rows],
            send_sem=part_send.at[c, k], recv_sem=part_recv.at[c, k],
            device_id=(v, (b + k) % bricks), device_id_type=MESH,
        )

    def composite(c):
        rows = pl.ds(c * RC, RC)
        transmit = jnp.ones((RC, 1, C), F32)
        colour = jnp.zeros((RC, 4, C), F32)
        for m in range(S):
            em = marched(emit, rows, m)
            opacity, e = one_minus_exp(em[:, 0:1, :])
            colour = colour + (transmit * opacity) * em
            transmit = transmit * e
        part[b, rows] = jnp.where(chan == 0, transmit, colour)

    def cot_copy(k, brick):
        rows = pl.ds(brick * RB, RB)
        return pltpu.make_async_remote_copy(
            src_ref=cots.at[rows], dst_ref=cots.at[rows],
            send_sem=cot_send.at[k], recv_sem=cot_recv.at[k],
            device_id=(v, (b + k) % bricks), device_id_type=MESH,
        )

    def halo_copy():
        return pltpu.make_async_remote_copy(
            src_ref=vol.at[0], dst_ref=halo, send_sem=halo_sems.at[0], recv_sem=halo_sems.at[1],
            device_id=(v, (b + bricks - 1) % bricks), device_id_type=MESH,
        )

    for s in range(S - 1):
        resample(s)

    ahead = nch // 2
    for s in range(S - 1):
        @pl.loop(0, ahead)
        def _(c, s=s):
            forward(s, c)

    pl.semaphore_wait(barrier, N - 1)

    @pl.when(b > 0)
    def _():
        halo_copy().start()

    for k in range(1, bricks):
        cot_copy(k, b).start()

    for s in range(S - 1):
        @pl.loop(ahead, nch)
        def _(c, s=s):
            forward(s, c)

    @pl.when(b == bricks - 1)
    def _():
        halo[...] = jnp.zeros_like(halo)

    @pl.when(b < bricks - 1)
    def _():
        halo_copy().wait_recv()

    resample(S - 1)

    @pl.loop(0, nch)
    def _(c):
        forward(S - 1, c)
        composite(c)
        for k in range(1, bricks):
            part_copy(c, k, b).start()

    for k in range(1, bricks):
        cot_copy(k, (b + bricks - k) % bricks).wait_recv()
    grads[...] = jnp.zeros_like(grads)
    position = jnp.where(back, bricks - 1 - b, b)

    def ordered(rows, p):
        return jnp.where(back, part[bricks - 1 - p, rows], part[p, rows])

    @pl.loop(0, nch)
    def _(c):
        rows = pl.ds(c * RC, RC)
        for k in range(1, bricks):
            part_copy(c, k, (b + bricks - k) % bricks).wait_recv()
        front = jnp.ones((RC, 1, C), F32)
        behind = jnp.zeros((RC, 4, C), F32)
        for p in range(bricks - 1):
            front = jnp.where(p < position, front * ordered(rows, p)[:, 0:1, :], front)
        for p in reversed(range(1, bricks)):
            here = ordered(rows, p)
            behind = jnp.where(p > position, here + here[:, 0:1, :] * behind, behind)
        grad = cots[rows] * front
        behind = jnp.sum(jnp.where(chan == 0, 0.0, grad * behind), 1, keepdims=True)
        transmit = jnp.ones((RC, 1, C), F32)
        steps = []
        for m in range(S):
            em = marched(emit, rows, m)
            opacity, e = one_minus_exp(em[:, 0:1, :])
            steps.append((em, marched(gate, rows, m), transmit * opacity, transmit * e))
            transmit = transmit * e
        tail = behind * transmit
        draws = [None] * S
        for m in reversed(range(S)):
            em, sg, weight, later = steps[m]
            q = jnp.sum(jnp.where(chan == 0, 0.0, grad * em), 1, keepdims=True)
            d_optical = q * later - tail
            tail = tail + q * weight
            draws[m] = jnp.where(chan == 0, d_optical * STEP_DEPTH * sg, grad * weight * (sg * (1.0 - sg)))
        for s in range(S):
            draw = jnp.where(back, draws[S - 1 - s], draws[s])
            draw = jnp.concatenate([draw[i] for i in range(RC)], 1)
            draw = jnp.concatenate([draw, jnp.zeros_like(draw)], 0)
            high = draw.astype(BF16).astype(F32)
            low = draw - high
            d_raw = jnp.concatenate([high, low, high, jnp.zeros_like(high)], 0).astype(BF16)
            g_out = blocks(d_raw[:2 * TILE], h2[s, c])
            du2 = dot(wob_s[...], d_raw) * d2[s, c]
            both = jnp.concatenate(split(du2), 0)
            g_mid = blocks(h1[s, c], both)
            du1 = dot_stacked(wmb_s[...], both) * d1[s, c]
            g_in = blocks(feats[s, c], jnp.concatenate(split(du1), 0))
            grads[0:2] += g_in.reshape(2, TILE, hid)
            grads[2:T - 1] += g_mid.reshape(T - 3, TILE, hid)
            grads[T - 1] += g_out

    def owner(t):
        return (t * N) // T

    def tile_copy(t, slot):
        return pltpu.make_async_remote_copy(
            src_ref=grads.at[t], dst_ref=landed.at[slot],
            send_sem=tile_send.at[t], recv_sem=tile_recv.at[slot],
            device_id=place(owner(t)), device_id_type=MESH,
        )

    def last_copy(t, k):
        return pltpu.make_async_remote_copy(
            src_ref=final.at[t], dst_ref=final.at[t],
            send_sem=last_send.at[k], recv_sem=last_recv.at[t],
            device_id=place((me + k) % N), device_id_type=MESH,
        )

    @pl.loop(0, T)
    def _(t):
        @pl.when(owner(t) != me)
        def _():
            tile_copy(t, (me - owner(t) + N - 1) % N).start()

    own = pl.ds(b * RB, RB)
    transmit = jnp.ones((RB, 1, C), F32)
    colour = jnp.zeros((RB, 4, C), F32)
    for p in range(bricks):
        here = ordered(own, p)
        colour = colour + transmit * here
        transmit = transmit * here[:, 0:1, :]
    for i in range(RB):
        for c in range(3):
            image[0, c, pl.ds(i, 1), :] = colour[i, 1 + c:2 + c, :]

    my_tile = (me * T + N - 1) // N
    owns = owner(my_tile) == me

    @pl.when(owns)
    def _():
        @pl.loop(0, N - 1)
        def _(k):
            tile_copy(my_tile, k).wait_recv()

        final[my_tile] = grads[my_tile] + jnp.sum(landed[...], 0)

        @pl.loop(1, N)
        def _(k):
            last_copy(my_tile, k).start()

    @pl.when(b > 0)
    def _():
        halo_copy().wait_send()

    for k in range(1, bricks):
        cot_copy(k, b).wait_send()

    @pl.loop(0, nch)
    def _(c):
        for k in range(1, bricks):
            part_copy(c, k, b).wait_send()

    @pl.loop(0, T)
    def _(t):
        @pl.when(owner(t) != me)
        def _():
            tile_copy(t, 0).wait_send()
            last_copy(t, 1).wait_recv()

    final_out[...] = final[...]

    @pl.when(owns)
    def _():
        @pl.loop(1, N)
        def _(k):
            last_copy(my_tile, k).wait_send()


def deliver(picture, tiles, image, out_in, out_mid, out_out):
    T, _, hid = tiles.shape
    image[...] = picture[...]
    out_in[...] = tiles[0:2].reshape(2 * TILE, hid)
    out_mid[...] = tiles[2:T - 1].reshape(hid, hid)
    out_out[...] = tiles[T - 1][:4]


def per_device(volume, offsets, shifts, order, cond, w_in, w_mid, w_out, cot_image):
    views, bricks = lax.axis_size("view"), lax.axis_size("brick")
    N = views * bricks
    S, CH, R, C = volume.shape
    RB = cot_image.shape[2]
    fin, hid = w_in.shape
    RC = min(8, R)
    nch = R // RC
    n = RC * C
    T = (fin + hid) // TILE + 1
    vmem = pl.BlockSpec(memory_space=pltpu.VMEM)
    smem = pl.BlockSpec(memory_space=pltpu.SMEM)
    kept = lambda rows, kind: pltpu.VMEM((S, nch, rows, n), kind)
    dma = lambda *shape: pltpu.SemaphoreType.DMA(shape)
    image, tiles = pl.pallas_call(
        functools.partial(kernel, views, bricks, S, R, C, RC, RB, hid),
        out_shape=(
            jax.ShapeDtypeStruct((1, 3, RB, C), F32),
            jax.ShapeDtypeStruct((T, TILE, hid), F32),
        ),
        in_specs=[vmem, smem, smem, smem, smem, vmem, vmem, vmem, vmem],
        out_specs=(vmem, vmem),
        scratch_shapes=[
            pltpu.VMEM((CH * R, C), F32),
            pltpu.VMEM((S, 2 * R + 1, CH, C), F32),
            kept(2 * fin, BF16), kept(2 * hid, BF16), kept(hid, F32), kept(2 * hid, BF16), kept(hid, F32),
            pltpu.VMEM((S, R, 4, C), F32),
            pltpu.VMEM((S, R, 4, C), F32),
            pltpu.VMEM((bricks, R, 4, C), F32),
            pltpu.VMEM((R, 4, C), F32),
            pltpu.VMEM((hid, 3 * fin), BF16),
            pltpu.VMEM((2 * hid, 2 * hid), BF16),
            pltpu.VMEM((2 * TILE, 2 * hid), BF16),
            pltpu.VMEM((2 * hid, 2 * hid), BF16),
            pltpu.VMEM((hid, 4 * TILE), BF16),
            pltpu.VMEM((T, TILE, hid), F32),
            pltpu.VMEM((N - 1, TILE, hid), F32),
            pltpu.VMEM((T, TILE, hid), F32),
            dma(2), dma(bricks), dma(bricks), dma(nch, bricks), dma(nch, bricks),
            dma(T), dma(N - 1), dma(N), dma(T),
        ],
        compiler_params=pltpu.CompilerParams(
            collective_id=0, has_side_effects=True, vmem_limit_bytes=40 * 1024 * 1024
        ),
        cost_estimate=pl.CostEstimate(
            flops=2 * S * R * C * hid * (3 * hid + 3 * fin + 12), bytes_accessed=4 * volume.size,
            transcendentals=2 * S * R * C * hid,
        ),
    )(volume.reshape(S, CH * R, C), offsets, shifts, order, cond, w_in, w_mid, w_out.T, cot_image)
    image, g_in, g_mid, g_out = pl.pallas_call(
        deliver,
        out_shape=(
            jax.ShapeDtypeStruct((1, 3, RB, C), F32),
            jax.ShapeDtypeStruct((fin, hid), F32),
            jax.ShapeDtypeStruct((hid, hid), F32),
            jax.ShapeDtypeStruct((4, hid), F32),
        ),
        in_specs=[vmem, vmem],
        out_specs=(vmem, vmem, vmem, vmem),
        compiler_params=pltpu.CompilerParams(vmem_limit_bytes=4 * 1024 * 1024),
    )(image, tiles)
    return image, g_in, g_mid, g_out.T


def solution(mesh):
    placed = (
        P("brick", None, None, None),
        P("view", None),
        P("view", None),
        P("view"),
        P("view", None),
        P(),
        P(),
        P(),
        P("view", None, "brick", None),
    )
    return jax.shard_map(
        per_device,
        mesh=mesh,
        in_specs=placed,
        out_specs=(P("view", None, "brick", None), P(), P(), P()),
        check_vma=False,
    )
```

```python
import functools

import jax
import jax.numpy as jnp
from jax import lax
from jax.experimental import pallas as pl
from jax.experimental.pallas import tpu as pltpu
from jax.sharding import PartitionSpec as P

STEP_DEPTH = 0.15
MESH = pl.DeviceIdType.MESH
F32 = jnp.float32
BF16 = jnp.bfloat16
TILE = 8


def split(x):
    high = x.astype(BF16)
    return high, (x - high.astype(F32)).astype(BF16)


def dot(a, b):
    return lax.dot_general(a, b, (((1,), (0,)), ((), ())), preferred_element_type=F32)


def stacked(high, low):
    return jnp.concatenate([jnp.concatenate([high, high], 1), jnp.concatenate([low, low], 1)], 0)


def dot_stacked(a, b):
    out = dot(a, b)
    rows = out.shape[0] // 2
    return out[:rows] + out[rows:]


def blocks(a, b):
    out = lax.dot_general(a, b, (((1,), (1,)), ((), ())), preferred_element_type=F32)
    rows, cols = out.shape[0] // 2, out.shape[1] // 2
    return (out[rows:, cols:] + out[rows:, :cols] + out[:rows, cols:]) + out[:rows, :cols]


def staggered(parts):
    waiting, active = list(parts), []
    while waiting or active:
        if waiting:
            active.append(waiting.pop(0))
        active = [part for part in active if next(part, part) is not part]


def activate(u):
    gate = 0.5 * jnp.tanh(0.5 * u) + 0.5
    h = u * gate
    return h, gate + h * (1.0 - gate)


def one_minus_exp(x):
    series = x * (1.0 - x * (1 / 2) * (1.0 - x * (1 / 3) * (1.0 - x * (1 / 4) * (1.0 - x * (1 / 5)))))
    e = jnp.exp(-x)
    return jnp.where(x < 0.0625, series, 1.0 - e), e


def kernel(
    views, bricks, S, R, C, RC, RB, hid,
    vol_far, offsets, shifts, order, cond, w_in_far, w_mid_far, w_out_far, cot_far,
    image, final_out,
    vol, w_in, w_mid, w_out, cot, in_sems,
    halo, shifted, feats, h1, d1, h2, d2, du2s, du1s, emit, gate, part, cots,
    wi_s, wm_s, wo_s, wmb_s, wob_s, grads, landed, final,
    halo_sems, cot_send, cot_recv, part_send, part_recv, tile_send, tile_recv, last_send, last_recv,
):
    CH = 8
    N = views * bricks
    T = grads.shape[0]
    nch = R // RC
    n = RC * C
    SUB = min(2 * C, n)
    v = lax.axis_index("view")
    b = lax.axis_index("brick")
    me = v * bricks + b

    def place(k):
        return (k // bricks, k % bricks)

    arrive = [
        pltpu.make_async_copy(far, near, in_sems.at[i])
        for i, (far, near) in enumerate(
            ((vol_far, vol), (w_in_far, w_in), (w_mid_far, w_mid), (w_out_far, w_out), (cot_far, cot))
        )
    ]
    for copy in arrive:
        copy.start()

    barrier = pltpu.get_barrier_semaphore()

    @pl.loop(1, N)
    def _(k):
        pl.semaphore_signal(barrier, inc=1, device_id=place((me + k) % N), device_id_type=MESH)

    f0, f1, f2 = offsets[0, 0], offsets[0, 1], offsets[0, 2]
    s0 = lax.rem(shifts[0, 0], R)
    s1 = lax.rem(shifts[0, 1], C)
    back = order[0] == 1

    for copy in arrive:
        copy.wait()

    for i in range(RB):
        cots[b * RB + i, pl.ds(0, 1), :] = jnp.zeros((1, C), F32)
        for c in range(3):
            cots[b * RB + i, pl.ds(1 + c, 1), :] = cot[0, c, pl.ds(i, 1), :]

    wi_hi, wi_lo = split(w_in[...].T)
    wi_s[...] = jnp.concatenate([wi_hi.astype(F32), wi_hi.astype(F32), wi_lo.astype(F32)], 1).astype(BF16)
    wm_hi, wm_lo = split(w_mid[...].T)
    wm_s[...] = stacked(wm_hi, wm_lo)
    wmb_hi, wmb_lo = split(w_mid[...])
    wmb_s[...] = stacked(wmb_hi, wmb_lo)
    wo_t = jnp.concatenate([w_out[...], jnp.zeros_like(w_out)], 0)
    wo_hi = wo_t.astype(BF16).astype(F32)
    wo_lo = wo_t - wo_hi
    wo_s[...] = stacked(wo_hi, wo_lo).astype(BF16)
    wob_s[...] = jnp.concatenate([wo_hi, wo_hi, wo_lo, jnp.zeros_like(wo_lo)], 0).T.astype(BF16)

    def resample(s):
        for i in range(R):
            near = vol[s, pl.ds(i, CH, stride=R), :]
            far = vol[s + 1, pl.ds(i, CH, stride=R), :] if s + 1 < S else halo[pl.ds(i, CH, stride=R), :]
            deep = (1.0 - f2) * near + f2 * far
            first = pltpu.roll(deep, lax.rem(C - s1, C), 1)
            second = pltpu.roll(deep, lax.rem(2 * C - 1 - s1, C), 1)
            mixed = (1.0 - f1) * first + f1 * second
            shifted[s, i] = mixed
            shifted[s, R + i] = mixed
            if i == 0:
                shifted[s, 2 * R] = mixed

    row = lax.broadcasted_iota(jnp.int32, (CH, SUB), 0)
    cond_rows = jnp.zeros((CH, SUB), F32)
    for c in range(CH):
        cond_rows = jnp.where(row == c, cond[0, c], cond_rows)
    chan = lax.broadcasted_iota(jnp.int32, (RC, 4, C), 1)

    def forward_part(s, c, j, mixed, raws):
        here = (s, c, slice(None), pl.ds(j * SUB, SUB))
        rows = range(j * SUB // C, (j + 1) * SUB // C)
        feat = jnp.concatenate([jnp.concatenate([mixed[i] for i in rows], 1), cond_rows], 0)
        hi, lo = split(feat)
        feats[here] = jnp.concatenate([hi, lo], 0)
        u = dot(wi_s[...], jnp.concatenate([hi, lo, hi], 0))
        yield
        h, d1[here] = activate(u)
        both = jnp.concatenate(split(h), 0)
        h1[here] = both
        u = dot_stacked(wm_s[...], both)
        yield
        h, d2[here] = activate(u)
        both = jnp.concatenate(split(h), 0)
        h2[here] = both
        raws[j] = dot_stacked(wo_s[...], both)
        yield

    def forward(s, c):
        rows = shifted[s, pl.ds(s0 + c * RC, RC + 1)]
        mixed = (1.0 - f0) * rows[:-1] + f0 * rows[1:]
        raws = [None] * (n // SUB)
        staggered([forward_part(s, c, j, mixed, raws) for j in range(n // SUB)])
        raw = jnp.concatenate(raws, 1)
        x = jnp.stack([raw[:4, i * C:(i + 1) * C] for i in range(RC)], 0)
        e = jnp.exp(-jnp.abs(x))
        r = 1.0 / (1.0 + e)
        sg = jnp.where(x >= 0, r, e * r)
        log1p = jnp.where(
            e < 0.0625, e * (1.0 - e * (1 / 2 - e * (1 / 3 - e * (1 / 4 - e * (1 / 5 - e * (1 / 6)))))), jnp.log(1.0 + e)
        )
        sp = jnp.maximum(x, 0.0) + log1p
        gate[s, pl.ds(c * RC, RC)] = sg
        emit[s, pl.ds(c * RC, RC)] = jnp.where(chan == 0, STEP_DEPTH * sp, sg)

    def marched(ref, rows, m):
        return jnp.where(back, ref[S - 1 - m, rows], ref[m, rows])

    def part_copy(c, k, brick):
        rows = pl.ds(c * RC, RC)
        return pltpu.make_async_remote_copy(
            src_ref=part.at[brick, rows], dst_ref=part.at[brick, rows],
            send_sem=part_send.at[c, k], recv_sem=part_recv.at[c, k],
            device_id=(v, (b + k) % bricks), device_id_type=MESH,
        )

    def composite(c):
        rows = pl.ds(c * RC, RC)
        transmit = jnp.ones((RC, 1, C), F32)
        colour = jnp.zeros((RC, 4, C), F32)
        for m in range(S):
            em = marched(emit, rows, m)
            opacity, e = one_minus_exp(em[:, 0:1, :])
            colour = colour + (transmit * opacity) * em
            transmit = transmit * e
        part[b, rows] = jnp.where(chan == 0, transmit, colour)

    def cot_copy(k, brick):
        rows = pl.ds(brick * RB, RB)
        return pltpu.make_async_remote_copy(
            src_ref=cots.at[rows], dst_ref=cots.at[rows],
            send_sem=cot_send.at[k], recv_sem=cot_recv.at[k],
            device_id=(v, (b + k) % bricks), device_id_type=MESH,
        )

    def halo_copy():
        return pltpu.make_async_remote_copy(
            src_ref=vol.at[0], dst_ref=halo, send_sem=halo_sems.at[0], recv_sem=halo_sems.at[1],
            device_id=(v, (b + bricks - 1) % bricks), device_id_type=MESH,
        )

    for s in range(S - 1):
        resample(s)

    ahead = nch // 2
    for s in range(S - 1):
        @pl.loop(0, ahead)
        def _(c, s=s):
            forward(s, c)

    pl.semaphore_wait(barrier, N - 1)

    @pl.when(b > 0)
    def _():
        halo_copy().start()

    for k in range(1, bricks):
        cot_copy(k, b).start()

    for s in range(S - 1):
        @pl.loop(ahead, nch)
        def _(c, s=s):
            forward(s, c)

    @pl.when(b == bricks - 1)
    def _():
        halo[...] = jnp.zeros_like(halo)

    @pl.when(b < bricks - 1)
    def _():
        halo_copy().wait_recv()

    resample(S - 1)

    @pl.loop(0, nch)
    def _(c):
        forward(S - 1, c)
        composite(c)
        for k in range(1, bricks):
            part_copy(c, k, b).start()

    for k in range(1, bricks):
        cot_copy(k, (b + bricks - k) % bricks).wait_recv()
    grads[...] = jnp.zeros_like(grads)
    position = jnp.where(back, bricks - 1 - b, b)

    def ordered(rows, p):
        return jnp.where(back, part[bricks - 1 - p, rows], part[p, rows])

    def backward_part(s, c, j, d_raw):
        lanes = pl.ds(j * SUB, SUB)
        u = dot(wob_s[...], d_raw[:, j * SUB:(j + 1) * SUB])
        yield
        both = jnp.concatenate(split(u * d2[s, c, :, lanes]), 0)
        du2s[s, :, lanes] = both
        u = dot_stacked(wmb_s[...], both)
        yield
        du1s[s, :, lanes] = jnp.concatenate(split(u * d1[s, c, :, lanes]), 0)
        yield

    @pl.loop(0, nch)
    def _(c):
        rows = pl.ds(c * RC, RC)
        for k in range(1, bricks):
            part_copy(c, k, (b + bricks - k) % bricks).wait_recv()
        front = jnp.ones((RC, 1, C), F32)
        behind = jnp.zeros((RC, 4, C), F32)
        for p in range(bricks - 1):
            front = jnp.where(p < position, front * ordered(rows, p)[:, 0:1, :], front)
        for p in reversed(range(1, bricks)):
            here = ordered(rows, p)
            behind = jnp.where(p > position, here + here[:, 0:1, :] * behind, behind)
        grad = cots[rows] * front
        behind = jnp.sum(jnp.where(chan == 0, 0.0, grad * behind), 1, keepdims=True)
        transmit = jnp.ones((RC, 1, C), F32)
        steps = []
        for m in range(S):
            em = marched(emit, rows, m)
            opacity, e = one_minus_exp(em[:, 0:1, :])
            steps.append((em, marched(gate, rows, m), transmit * opacity, transmit * e))
            transmit = transmit * e
        tail = behind * transmit
        draws = [None] * S
        for m in reversed(range(S)):
            em, sg, weight, later = steps[m]
            q = jnp.sum(jnp.where(chan == 0, 0.0, grad * em), 1, keepdims=True)
            d_optical = q * later - tail
            tail = tail + q * weight
            draws[m] = jnp.where(chan == 0, d_optical * STEP_DEPTH * sg, grad * weight * (sg * (1.0 - sg)))
        parts, d_raws = [], []
        for s in range(S):
            draw = jnp.where(back, draws[S - 1 - s], draws[s])
            draw = jnp.concatenate([draw[i] for i in range(RC)], 1)
            draw = jnp.concatenate([draw, jnp.zeros_like(draw)], 0)
            high = draw.astype(BF16).astype(F32)
            low = draw - high
            d_raw = jnp.concatenate([high, low, high, jnp.zeros_like(high)], 0).astype(BF16)
            d_raws.append(d_raw)
            parts += [backward_part(s, c, j, d_raw) for j in range(n // SUB)]
        staggered(parts)
        for s in range(S):
            g_out = blocks(d_raws[s][:2 * TILE], h2[s, c])
            g_mid = blocks(h1[s, c], du2s[s])
            g_in = blocks(feats[s, c], du1s[s])
            grads[0:2] += g_in.reshape(2, TILE, hid)
            grads[2:T - 1] += g_mid.reshape(T - 3, TILE, hid)
            grads[T - 1] += g_out

    def owner(t):
        return (t * N) // T

    def tile_copy(t, slot):
        return pltpu.make_async_remote_copy(
            src_ref=grads.at[t], dst_ref=landed.at[slot],
            send_sem=tile_send.at[t], recv_sem=tile_recv.at[slot],
            device_id=place(owner(t)), device_id_type=MESH,
        )

    def last_copy(t, k):
        return pltpu.make_async_remote_copy(
            src_ref=final.at[t], dst_ref=final.at[t],
            send_sem=last_send.at[k], recv_sem=last_recv.at[t],
            device_id=place((me + k) % N), device_id_type=MESH,
        )

    @pl.loop(0, T)
    def _(t):
        @pl.when(owner(t) != me)
        def _():
            tile_copy(t, (me - owner(t) + N - 1) % N).start()

    own = pl.ds(b * RB, RB)
    transmit = jnp.ones((RB, 1, C), F32)
    colour = jnp.zeros((RB, 4, C), F32)
    for p in range(bricks):
        here = ordered(own, p)
        colour = colour + transmit * here
        transmit = transmit * here[:, 0:1, :]
    for i in range(RB):
        for c in range(3):
            image[0, c, pl.ds(i, 1), :] = colour[i, 1 + c:2 + c, :]

    my_tile = (me * T + N - 1) // N
    owns = owner(my_tile) == me

    @pl.when(owns)
    def _():
        @pl.loop(0, N - 1)
        def _(k):
            tile_copy(my_tile, k).wait_recv()

        final[my_tile] = grads[my_tile] + jnp.sum(landed[...], 0)

        @pl.loop(1, N)
        def _(k):
            last_copy(my_tile, k).start()

    @pl.when(b > 0)
    def _():
        halo_copy().wait_send()

    for k in range(1, bricks):
        cot_copy(k, b).wait_send()

    @pl.loop(0, nch)
    def _(c):
        for k in range(1, bricks):
            part_copy(c, k, b).wait_send()

    @pl.loop(0, T)
    def _(t):
        @pl.when(owner(t) != me)
        def _():
            tile_copy(t, 0).wait_send()
            last_copy(t, 1).wait_recv()

    final_out[...] = final[...].reshape(final_out.shape)

    @pl.when(owns)
    def _():
        @pl.loop(1, N)
        def _(k):
            last_copy(my_tile, k).wait_send()


def deliver(picture, tiles, image, out_in, out_mid, out_out, sems):
    fin, hid = out_in.shape[0], out_mid.shape[0]
    copies = [
        pltpu.make_async_copy(source, target, sems.at[i])
        for i, (source, target) in enumerate(
            (
                (tiles.at[pl.ds(fin, hid)], out_mid),
                (picture, image),
                (tiles.at[pl.ds(0, fin)], out_in),
                (tiles.at[pl.ds(fin + hid, 4)], out_out),
            )
        )
    ]
    for copy in copies:
        copy.start()
    for copy in copies:
        copy.wait()


def per_device(volume, offsets, shifts, order, cond, w_in, w_mid, w_out, cot_image):
    views, bricks = lax.axis_size("view"), lax.axis_size("brick")
    N = views * bricks
    S, CH, R, C = volume.shape
    RB = cot_image.shape[2]
    fin, hid = w_in.shape
    RC = min(8, R)
    nch = R // RC
    n = RC * C
    T = (fin + hid) // TILE + 1
    vmem = pl.BlockSpec(memory_space=pltpu.VMEM)
    far = pl.BlockSpec(memory_space=pltpu.HBM)
    smem = pl.BlockSpec(memory_space=pltpu.SMEM)
    kept = lambda rows, kind: pltpu.VMEM((S, nch, rows, n), kind)
    dma = lambda *shape: pltpu.SemaphoreType.DMA(shape)
    image, tiles = pl.pallas_call(
        functools.partial(kernel, views, bricks, S, R, C, RC, RB, hid),
        out_shape=(
            jax.ShapeDtypeStruct((1, 3, RB, C), F32),
            jax.ShapeDtypeStruct((T * TILE, hid), F32),
        ),
        in_specs=[far, smem, smem, smem, smem, far, far, far, far],
        out_specs=(vmem, vmem),
        scratch_shapes=[
            pltpu.VMEM((S, CH * R, C), F32),
            pltpu.VMEM(w_in.shape, F32),
            pltpu.VMEM(w_mid.shape, F32),
            pltpu.VMEM(w_out.shape[::-1], F32),
            pltpu.VMEM(cot_image.shape, F32),
            dma(5),
            pltpu.VMEM((CH * R, C), F32),
            pltpu.VMEM((S, 2 * R + 1, CH, C), F32),
            kept(2 * fin, BF16), kept(2 * hid, BF16), kept(hid, F32), kept(2 * hid, BF16), kept(hid, F32),
            pltpu.VMEM((S, 2 * hid, n), BF16), pltpu.VMEM((S, 2 * hid, n), BF16),
            pltpu.VMEM((S, R, 4, C), F32),
            pltpu.VMEM((S, R, 4, C), F32),
            pltpu.VMEM((bricks, R, 4, C), F32),
            pltpu.VMEM((R, 4, C), F32),
            pltpu.VMEM((hid, 3 * fin), BF16),
            pltpu.VMEM((2 * hid, 2 * hid), BF16),
            pltpu.VMEM((2 * TILE, 2 * hid), BF16),
            pltpu.VMEM((2 * hid, 2 * hid), BF16),
            pltpu.VMEM((hid, 4 * TILE), BF16),
            pltpu.VMEM((T, TILE, hid), F32),
            pltpu.VMEM((N - 1, TILE, hid), F32),
            pltpu.VMEM((T, TILE, hid), F32),
            dma(2), dma(bricks), dma(bricks), dma(nch, bricks), dma(nch, bricks),
            dma(T), dma(N - 1), dma(N), dma(T),
        ],
        compiler_params=pltpu.CompilerParams(
            collective_id=0, has_side_effects=True, vmem_limit_bytes=60 * 1024 * 1024
        ),
        cost_estimate=pl.CostEstimate(
            flops=2 * S * R * C * hid * (3 * hid + 3 * fin + 12), bytes_accessed=4 * volume.size,
            transcendentals=2 * S * R * C * hid,
        ),
    )(volume.reshape(S, CH * R, C), offsets, shifts, order, cond, w_in, w_mid, w_out.T, cot_image)
    image, g_in, g_mid, g_out = pl.pallas_call(
        deliver,
        out_shape=(
            jax.ShapeDtypeStruct((1, 3, RB, C), F32),
            jax.ShapeDtypeStruct((fin, hid), F32),
            jax.ShapeDtypeStruct((hid, hid), F32),
            jax.ShapeDtypeStruct((4, hid), F32),
        ),
        in_specs=[far, far],
        out_specs=(far, far, far, far),
        scratch_shapes=[dma(4)],
        compiler_params=pltpu.CompilerParams(vmem_limit_bytes=60 * 1024 * 1024),
    )(image, tiles)
    return image, g_in, g_mid, g_out.T


def solution(mesh):
    placed = (
        P("brick", None, None, None),
        P("view", None),
        P("view", None),
        P("view"),
        P("view", None),
        P(),
        P(),
        P(),
        P("view", None, "brick", None),
    )
    return jax.shard_map(
        per_device,
        mesh=mesh,
        in_specs=placed,
        out_specs=(P("view", None, "brick", None), P(), P(), P()),
        check_vma=False,
    )
```

```python
import functools

import jax
import jax.numpy as jnp
from jax import lax
from jax.experimental import pallas as pl
from jax.experimental.pallas import tpu as pltpu
from jax.sharding import PartitionSpec as P

STEP_DEPTH = 0.15
MESH = pl.DeviceIdType.MESH
F32 = jnp.float32
BF16 = jnp.bfloat16
TILE = 8


def split(x):
    high = x.astype(BF16)
    return high, (x - high.astype(F32)).astype(BF16)


def dot(a, b):
    return lax.dot_general(a, b, (((1,), (0,)), ((), ())), preferred_element_type=F32)


def stacked(high, low):
    return jnp.concatenate([jnp.concatenate([high, high], 1), jnp.concatenate([low, low], 1)], 0)


def dot_stacked(a, b):
    out = dot(a, b)
    rows = out.shape[0] // 2
    return out[:rows] + out[rows:]


def blocks(a, b):
    out = lax.dot_general(a, b, (((1,), (1,)), ((), ())), preferred_element_type=F32)
    rows, cols = out.shape[0] // 2, out.shape[1] // 2
    return (out[rows:, cols:] + out[rows:, :cols] + out[:rows, cols:]) + out[:rows, :cols]


def activate(u):
    gate = 0.5 * jnp.tanh(0.5 * u) + 0.5
    h = u * gate
    return h, gate + h * (1.0 - gate)


def one_minus_exp(x):
    series = x * (1.0 - x * (1 / 2) * (1.0 - x * (1 / 3) * (1.0 - x * (1 / 4) * (1.0 - x * (1 / 5)))))
    e = jnp.exp(-x)
    return jnp.where(x < 0.0625, series, 1.0 - e), e


def kernel(
    views, bricks, S, R, C, RC, RB, hid,
    vol_far, offsets, shifts, order, cond, w_in_far, w_mid_far, w_out_far, cot_far,
    image, final_out,
    vol, w_in, w_mid, w_out, cot, in_sems,
    halo, shifted, feats, h1, d1, h2, d2, emit, gate, part, cots,
    wi_s, wm_s, wo_s, wmb_s, wob_s, grads, sum_in, sum_out, landed, final,
    halo_sems, cot_send, cot_recv, part_send, part_recv, tile_send, tile_recv, last_send, last_recv,
):
    CH = 8
    N = views * bricks
    T = grads.shape[0]
    nch = R // RC
    n = RC * C
    v = lax.axis_index("view")
    b = lax.axis_index("brick")
    me = v * bricks + b

    def place(k):
        return (k // bricks, k % bricks)

    arrive = [
        pltpu.make_async_copy(far, near, in_sems.at[i])
        for i, (far, near) in enumerate(
            ((vol_far, vol), (w_in_far, w_in), (w_mid_far, w_mid), (w_out_far, w_out), (cot_far, cot))
        )
    ]
    for copy in arrive:
        copy.start()

    barrier = pltpu.get_barrier_semaphore()

    @pl.loop(1, N)
    def _(k):
        pl.semaphore_signal(barrier, inc=1, device_id=place((me + k) % N), device_id_type=MESH)

    f0, f1, f2 = offsets[0, 0], offsets[0, 1], offsets[0, 2]
    s0 = lax.rem(shifts[0, 0], R)
    s1 = lax.rem(shifts[0, 1], C)
    back = order[0] == 1

    for copy in arrive:
        copy.wait()

    for i in range(RB):
        cots[b * RB + i, pl.ds(0, 1), :] = jnp.zeros((1, C), F32)
        for c in range(3):
            cots[b * RB + i, pl.ds(1 + c, 1), :] = cot[0, c, pl.ds(i, 1), :]

    wi_hi, wi_lo = split(w_in[...].T)
    wi_s[...] = jnp.concatenate([wi_hi.astype(F32), wi_hi.astype(F32), wi_lo.astype(F32)], 1).astype(BF16)
    wm_hi, wm_lo = split(w_mid[...].T)
    wm_s[...] = stacked(wm_hi, wm_lo)
    wmb_hi, wmb_lo = split(w_mid[...])
    wmb_s[...] = stacked(wmb_hi, wmb_lo)
    wo_t = jnp.concatenate([w_out[...], jnp.zeros_like(w_out)], 0)
    wo_hi = wo_t.astype(BF16).astype(F32)
    wo_lo = wo_t - wo_hi
    wo_s[...] = stacked(wo_hi, wo_lo).astype(BF16)
    wob_s[...] = jnp.concatenate([wo_hi, wo_hi, wo_lo, jnp.zeros_like(wo_lo)], 0).T.astype(BF16)

    def resample(s):
        for i in range(R):
            near = vol[s, pl.ds(i, CH, stride=R), :]
            far = vol[s + 1, pl.ds(i, CH, stride=R), :] if s + 1 < S else halo[pl.ds(i, CH, stride=R), :]
            deep = (1.0 - f2) * near + f2 * far
            first = pltpu.roll(deep, lax.rem(C - s1, C), 1)
            second = pltpu.roll(deep, lax.rem(2 * C - 1 - s1, C), 1)
            mixed = (1.0 - f1) * first + f1 * second
            shifted[s, i] = mixed
            shifted[s, R + i] = mixed
            if i == 0:
                shifted[s, 2 * R] = mixed

    row = lax.broadcasted_iota(jnp.int32, (CH, n), 0)
    cond_rows = jnp.zeros((CH, n), F32)
    for c in range(CH):
        cond_rows = jnp.where(row == c, cond[0, c], cond_rows)
    chan = lax.broadcasted_iota(jnp.int32, (RC, 4, C), 1)

    def forward(s, c):
        rows = shifted[s, pl.ds(s0 + c * RC, RC + 1)]
        mixed = (1.0 - f0) * rows[:-1] + f0 * rows[1:]
        feat = jnp.concatenate([jnp.concatenate([mixed[i] for i in range(RC)], 1), cond_rows], 0)
        hi, lo = split(feat)
        feats[s, c] = jnp.concatenate([hi, lo], 0)
        h, d = activate(dot(wi_s[...], jnp.concatenate([hi, lo, hi], 0)))
        d1[s, c] = d
        both = jnp.concatenate(split(h), 0)
        h1[s, c] = both
        h, d = activate(dot_stacked(wm_s[...], both))
        d2[s, c] = d
        both = jnp.concatenate(split(h), 0)
        h2[s, c] = both
        raw = dot_stacked(wo_s[...], both)
        x = jnp.stack([raw[:4, i * C:(i + 1) * C] for i in range(RC)], 0)
        e = jnp.exp(-jnp.abs(x))
        r = 1.0 / (1.0 + e)
        sg = jnp.where(x >= 0, r, e * r)
        log1p = jnp.where(
            e < 0.0625, e * (1.0 - e * (1 / 2 - e * (1 / 3 - e * (1 / 4 - e * (1 / 5 - e * (1 / 6)))))), jnp.log(1.0 + e)
        )
        sp = jnp.maximum(x, 0.0) + log1p
        gate[s, pl.ds(c * RC, RC)] = sg
        emit[s, pl.ds(c * RC, RC)] = jnp.where(chan == 0, STEP_DEPTH * sp, sg)

    def marched(ref, rows, m):
        return jnp.where(back, ref[S - 1 - m, rows], ref[m, rows])

    def part_copy(c, k, brick):
        rows = pl.ds(c * RC, RC)
        return pltpu.make_async_remote_copy(
            src_ref=part.at[brick, rows], dst_ref=part.at[brick, rows],
            send_sem=part_send.at[c, k], recv_sem=part_recv.at[c, k],
            device_id=(v, (b + k) % bricks), device_id_type=MESH,
        )

    def composite(c):
        rows = pl.ds(c * RC, RC)
        transmit = jnp.ones((RC, 1, C), F32)
        colour = jnp.zeros((RC, 4, C), F32)
        for m in range(S):
            em = marched(emit, rows, m)
            opacity, e = one_minus_exp(em[:, 0:1, :])
            colour = colour + (transmit * opacity) * em
            transmit = transmit * e
        part[b, rows] = jnp.where(chan == 0, transmit, colour)

    def cot_copy(k, brick):
        rows = pl.ds(brick * RB, RB)
        return pltpu.make_async_remote_copy(
            src_ref=cots.at[rows], dst_ref=cots.at[rows],
            send_sem=cot_send.at[k], recv_sem=cot_recv.at[k],
            device_id=(v, (b + k) % bricks), device_id_type=MESH,
        )

    def halo_copy():
        return pltpu.make_async_remote_copy(
            src_ref=vol.at[0], dst_ref=halo, send_sem=halo_sems.at[0], recv_sem=halo_sems.at[1],
            device_id=(v, (b + bricks - 1) % bricks), device_id_type=MESH,
        )

    for s in range(S - 1):
        resample(s)

    ahead = nch // 2
    for s in range(S - 1):
        @pl.loop(0, ahead)
        def _(c, s=s):
            forward(s, c)

    pl.semaphore_wait(barrier, N - 1)

    @pl.when(b > 0)
    def _():
        halo_copy().start()

    for k in range(1, bricks):
        cot_copy(k, b).start()

    for s in range(S - 1):
        @pl.loop(ahead, nch)
        def _(c, s=s):
            forward(s, c)

    @pl.when(b == bricks - 1)
    def _():
        halo[...] = jnp.zeros_like(halo)

    @pl.when(b < bricks - 1)
    def _():
        halo_copy().wait_recv()

    resample(S - 1)

    @pl.loop(0, nch)
    def _(c):
        forward(S - 1, c)
        composite(c)
        for k in range(1, bricks):
            part_copy(c, k, b).start()

    for k in range(1, bricks):
        cot_copy(k, (b + bricks - k) % bricks).wait_recv()
    grads[...] = jnp.zeros_like(grads)
    sum_in[...] = jnp.zeros_like(sum_in)
    sum_out[...] = jnp.zeros_like(sum_out)
    position = jnp.where(back, bricks - 1 - b, b)

    def ordered(rows, p):
        return jnp.where(back, part[bricks - 1 - p, rows], part[p, rows])

    @pl.loop(0, nch)
    def _(c):
        rows = pl.ds(c * RC, RC)
        for k in range(1, bricks):
            part_copy(c, k, (b + bricks - k) % bricks).wait_recv()
        front = jnp.ones((RC, 1, C), F32)
        behind = jnp.zeros((RC, 4, C), F32)
        for p in range(bricks - 1):
            front = jnp.where(p < position, front * ordered(rows, p)[:, 0:1, :], front)
        for p in reversed(range(1, bricks)):
            here = ordered(rows, p)
            behind = jnp.where(p > position, here + here[:, 0:1, :] * behind, behind)
        grad = cots[rows] * front
        behind = jnp.sum(jnp.where(chan == 0, 0.0, grad * behind), 1, keepdims=True)
        transmit = jnp.ones((RC, 1, C), F32)
        steps = []
        for m in range(S):
            em = marched(emit, rows, m)
            opacity, e = one_minus_exp(em[:, 0:1, :])
            steps.append((em, marched(gate, rows, m), transmit * opacity, transmit * e))
            transmit = transmit * e
        tail = behind * transmit
        draws = [None] * S
        for m in reversed(range(S)):
            em, sg, weight, later = steps[m]
            q = jnp.sum(jnp.where(chan == 0, 0.0, grad * em), 1, keepdims=True)
            d_optical = q * later - tail
            tail = tail + q * weight
            draws[m] = jnp.where(chan == 0, d_optical * STEP_DEPTH * sg, grad * weight * (sg * (1.0 - sg)))
        for s in range(S):
            draw = jnp.where(back, draws[S - 1 - s], draws[s])
            draw = jnp.concatenate([draw[i] for i in range(RC)], 1)
            draw = jnp.concatenate([draw, jnp.zeros_like(draw)], 0)
            high = draw.astype(BF16).astype(F32)
            low = draw - high
            d_raw = jnp.concatenate([high, low, high, jnp.zeros_like(high)], 0).astype(BF16)
            g_out = blocks(h2[s, c], d_raw[:2 * TILE])
            du2 = dot(wob_s[...], d_raw) * d2[s, c]
            both = jnp.concatenate(split(du2), 0)
            g_mid = blocks(h1[s, c], both)
            du1 = dot_stacked(wmb_s[...], both) * d1[s, c]
            g_in = blocks(jnp.concatenate(split(du1), 0), feats[s, c])
            sum_in[...] += g_in
            grads[2:T - 1] += g_mid.reshape(T - 3, TILE, hid)
            sum_out[...] += g_out

    grads[0:2] = sum_in[...].T.reshape(2, TILE, hid)
    grads[T - 1] = sum_out[...].T

    def owner(t):
        return (t * N) // T

    def tile_copy(t, slot):
        return pltpu.make_async_remote_copy(
            src_ref=grads.at[t], dst_ref=landed.at[slot],
            send_sem=tile_send.at[t], recv_sem=tile_recv.at[slot],
            device_id=place(owner(t)), device_id_type=MESH,
        )

    def last_copy(t, k):
        return pltpu.make_async_remote_copy(
            src_ref=final.at[t], dst_ref=final.at[t],
            send_sem=last_send.at[k], recv_sem=last_recv.at[t],
            device_id=place((me + k) % N), device_id_type=MESH,
        )

    @pl.loop(0, T)
    def _(t):
        @pl.when(owner(t) != me)
        def _():
            tile_copy(t, (me - owner(t) + N - 1) % N).start()

    own = pl.ds(b * RB, RB)
    transmit = jnp.ones((RB, 1, C), F32)
    colour = jnp.zeros((RB, 4, C), F32)
    for p in range(bricks):
        here = ordered(own, p)
        colour = colour + transmit * here
        transmit = transmit * here[:, 0:1, :]
    for i in range(RB):
        for c in range(3):
            image[0, c, pl.ds(i, 1), :] = colour[i, 1 + c:2 + c, :]

    my_tile = (me * T + N - 1) // N
    owns = owner(my_tile) == me

    @pl.when(owns)
    def _():
        @pl.loop(0, N - 1)
        def _(k):
            tile_copy(my_tile, k).wait_recv()

        final[my_tile] = grads[my_tile] + jnp.sum(landed[...], 0)

        @pl.loop(1, N)
        def _(k):
            last_copy(my_tile, k).start()

    @pl.when(b > 0)
    def _():
        halo_copy().wait_send()

    for k in range(1, bricks):
        cot_copy(k, b).wait_send()

    @pl.loop(0, nch)
    def _(c):
        for k in range(1, bricks):
            part_copy(c, k, b).wait_send()

    @pl.loop(0, T)
    def _(t):
        @pl.when(owner(t) != me)
        def _():
            tile_copy(t, 0).wait_send()
            last_copy(t, 1).wait_recv()

    final_out[...] = final[...]

    @pl.when(owns)
    def _():
        @pl.loop(1, N)
        def _(k):
            last_copy(my_tile, k).wait_send()


def deliver(picture, tiles, image, out_in, out_mid, out_out):
    T, _, hid = tiles.shape
    image[...] = picture[...]
    out_in[...] = tiles[0:2].reshape(2 * TILE, hid)
    out_mid[...] = tiles[2:T - 1].reshape(hid, hid)
    out_out[...] = tiles[T - 1][:4]


def per_device(volume, offsets, shifts, order, cond, w_in, w_mid, w_out, cot_image):
    views, bricks = lax.axis_size("view"), lax.axis_size("brick")
    N = views * bricks
    S, CH, R, C = volume.shape
    RB = cot_image.shape[2]
    fin, hid = w_in.shape
    RC = 16 if R % 16 == 0 else R
    nch = R // RC
    n = RC * C
    T = (fin + hid) // TILE + 1
    vmem = pl.BlockSpec(memory_space=pltpu.VMEM)
    far = pl.BlockSpec(memory_space=pltpu.HBM)
    smem = pl.BlockSpec(memory_space=pltpu.SMEM)
    kept = lambda rows, kind: pltpu.VMEM((S, nch, rows, n), kind)
    dma = lambda *shape: pltpu.SemaphoreType.DMA(shape)
    image, tiles = pl.pallas_call(
        functools.partial(kernel, views, bricks, S, R, C, RC, RB, hid),
        out_shape=(
            jax.ShapeDtypeStruct((1, 3, RB, C), F32),
            jax.ShapeDtypeStruct((T, TILE, hid), F32),
        ),
        in_specs=[far, smem, smem, smem, smem, far, far, far, far],
        out_specs=(vmem, vmem),
        scratch_shapes=[
            pltpu.VMEM((S, CH * R, C), F32),
            pltpu.VMEM(w_in.shape, F32),
            pltpu.VMEM(w_mid.shape, F32),
            pltpu.VMEM(w_out.shape[::-1], F32),
            pltpu.VMEM(cot_image.shape, F32),
            dma(5),
            pltpu.VMEM((CH * R, C), F32),
            pltpu.VMEM((S, 2 * R + 1, CH, C), F32),
            kept(2 * fin, BF16), kept(2 * hid, BF16), kept(hid, F32), kept(2 * hid, BF16), kept(hid, F32),
            pltpu.VMEM((S, R, 4, C), F32),
            pltpu.VMEM((S, R, 4, C), F32),
            pltpu.VMEM((bricks, R, 4, C), F32),
            pltpu.VMEM((R, 4, C), F32),
            pltpu.VMEM((hid, 3 * fin), BF16),
            pltpu.VMEM((2 * hid, 2 * hid), BF16),
            pltpu.VMEM((2 * TILE, 2 * hid), BF16),
            pltpu.VMEM((2 * hid, 2 * hid), BF16),
            pltpu.VMEM((hid, 4 * TILE), BF16),
            pltpu.VMEM((T, TILE, hid), F32),
            pltpu.VMEM((hid, fin), F32),
            pltpu.VMEM((hid, TILE), F32),
            pltpu.VMEM((N - 1, TILE, hid), F32),
            pltpu.VMEM((T, TILE, hid), F32),
            dma(2), dma(bricks), dma(bricks), dma(nch, bricks), dma(nch, bricks),
            dma(T), dma(N - 1), dma(N), dma(T),
        ],
        compiler_params=pltpu.CompilerParams(
            collective_id=0, has_side_effects=True, vmem_limit_bytes=60 * 1024 * 1024
        ),
        cost_estimate=pl.CostEstimate(
            flops=2 * S * R * C * hid * (3 * hid + 3 * fin + 12), bytes_accessed=4 * volume.size,
            transcendentals=2 * S * R * C * hid,
        ),
    )(volume.reshape(S, CH * R, C), offsets, shifts, order, cond, w_in, w_mid, w_out.T, cot_image)
    image, g_in, g_mid, g_out = pl.pallas_call(
        deliver,
        out_shape=(
            jax.ShapeDtypeStruct((1, 3, RB, C), F32),
            jax.ShapeDtypeStruct((fin, hid), F32),
            jax.ShapeDtypeStruct((hid, hid), F32),
            jax.ShapeDtypeStruct((4, hid), F32),
        ),
        in_specs=[vmem, vmem],
        out_specs=(vmem, vmem, vmem, vmem),
        compiler_params=pltpu.CompilerParams(vmem_limit_bytes=60 * 1024 * 1024),
    )(image, tiles)
    return image, g_in, g_mid, g_out.T


def solution(mesh):
    placed = (
        P("brick", None, None, None),
        P("view", None),
        P("view", None),
        P("view"),
        P("view", None),
        P(),
        P(),
        P(),
        P("view", None, "brick", None),
    )
    return jax.shard_map(
        per_device,
        mesh=mesh,
        in_specs=placed,
        out_specs=(P("view", None, "brick", None), P(), P(), P()),
        check_vma=False,
    )
```

```python
import functools

import jax
import jax.numpy as jnp
from jax import lax
from jax.experimental import pallas as pl
from jax.experimental.pallas import tpu as pltpu
from jax.sharding import PartitionSpec as P

STEP_DEPTH = 0.15
MESH = pl.DeviceIdType.MESH
F32 = jnp.float32
BF16 = jnp.bfloat16
TILE = 8


def split(x):
    high = x.astype(BF16)
    return high, (x - high.astype(F32)).astype(BF16)


def dot(a, b):
    return lax.dot_general(a, b, (((1,), (0,)), ((), ())), preferred_element_type=F32)


def stacked(high, low):
    return jnp.concatenate([jnp.concatenate([high, high], 1), jnp.concatenate([low, low], 1)], 0)


def dot_stacked(a, b):
    out = dot(a, b)
    rows = out.shape[0] // 2
    return out[:rows] + out[rows:]


def blocks(a, b):
    out = lax.dot_general(a, b, (((1,), (1,)), ((), ())), preferred_element_type=F32)
    rows, cols = out.shape[0] // 2, out.shape[1] // 2
    return (out[rows:, cols:] + out[rows:, :cols] + out[:rows, cols:]) + out[:rows, :cols]


def activate(u):
    gate = 0.5 * jnp.tanh(0.5 * u) + 0.5
    h = u * gate
    return h, gate + h * (1.0 - gate)


def one_minus_exp(x):
    series = x * (1.0 - x * (1 / 2) * (1.0 - x * (1 / 3) * (1.0 - x * (1 / 4) * (1.0 - x * (1 / 5)))))
    e = jnp.exp(-x)
    return jnp.where(x < 0.0625, series, 1.0 - e), e


def kernel(
    views, bricks, S, R, C, RC, RB, hid,
    vol_far, offsets, shifts, order, cond, w_in_far, w_mid_far, w_out_far, cot_far,
    image, final_out,
    vol, w_in, w_mid, w_out, cot, in_sems,
    halo, shifted, feats, h1, d1, h2, d2, emit, gate, part, cots,
    wi_s, wm_s, wo_s, wmb_s, wob_s, grads, sum_in, sum_out, landed, final,
    halo_sems, cot_send, cot_recv, part_send, part_recv, tile_send, tile_recv, last_send, last_recv,
):
    CH = 8
    N = views * bricks
    T = grads.shape[0]
    nch = R // RC
    n = RC * C
    v = lax.axis_index("view")
    b = lax.axis_index("brick")
    me = v * bricks + b

    def place(k):
        return (k // bricks, k % bricks)

    arrive = [
        pltpu.make_async_copy(far, near, in_sems.at[i])
        for i, (far, near) in enumerate(
            ((vol_far, vol), (w_in_far, w_in), (w_mid_far, w_mid), (w_out_far, w_out), (cot_far, cot))
        )
    ]
    for copy in arrive:
        copy.start()

    barrier = pltpu.get_barrier_semaphore()

    @pl.loop(1, N)
    def _(k):
        pl.semaphore_signal(barrier, inc=1, device_id=place((me + k) % N), device_id_type=MESH)

    f0, f1, f2 = offsets[0, 0], offsets[0, 1], offsets[0, 2]
    s0 = lax.rem(shifts[0, 0], R)
    s1 = lax.rem(shifts[0, 1], C)
    back = order[0] == 1

    for copy in arrive:
        copy.wait()

    for i in range(RB):
        cots[b * RB + i, pl.ds(0, 1), :] = jnp.zeros((1, C), F32)
        for c in range(3):
            cots[b * RB + i, pl.ds(1 + c, 1), :] = cot[0, c, pl.ds(i, 1), :]

    wi_hi, wi_lo = split(w_in[...].T)
    wi_s[...] = jnp.concatenate([wi_hi.astype(F32), wi_hi.astype(F32), wi_lo.astype(F32)], 1).astype(BF16)
    wm_hi, wm_lo = split(w_mid[...].T)
    wm_s[...] = stacked(wm_hi, wm_lo)
    wmb_hi, wmb_lo = split(w_mid[...])
    wmb_s[...] = stacked(wmb_hi, wmb_lo)
    wo_t = jnp.concatenate([w_out[...], jnp.zeros_like(w_out)], 0)
    wo_hi = wo_t.astype(BF16).astype(F32)
    wo_lo = wo_t - wo_hi
    wo_s[...] = stacked(wo_hi, wo_lo).astype(BF16)
    wob_s[...] = jnp.concatenate([wo_hi, wo_hi, wo_lo, jnp.zeros_like(wo_lo)], 0).T.astype(BF16)

    def resample(s):
        for i in range(R):
            near = vol[s, pl.ds(i, CH, stride=R), :]
            far = vol[s + 1, pl.ds(i, CH, stride=R), :] if s + 1 < S else halo[pl.ds(i, CH, stride=R), :]
            deep = (1.0 - f2) * near + f2 * far
            first = pltpu.roll(deep, lax.rem(C - s1, C), 1)
            second = pltpu.roll(deep, lax.rem(2 * C - 1 - s1, C), 1)
            mixed = (1.0 - f1) * first + f1 * second
            shifted[s, i] = mixed
            shifted[s, R + i] = mixed
            if i == 0:
                shifted[s, 2 * R] = mixed

    row = lax.broadcasted_iota(jnp.int32, (CH, n), 0)
    cond_rows = jnp.zeros((CH, n), F32)
    for c in range(CH):
        cond_rows = jnp.where(row == c, cond[0, c], cond_rows)
    chan = lax.broadcasted_iota(jnp.int32, (RC, 4, C), 1)

    def forward(s, c):
        rows = shifted[s, pl.ds(s0 + c * RC, RC + 1)]
        mixed = (1.0 - f0) * rows[:-1] + f0 * rows[1:]
        feat = jnp.concatenate([jnp.concatenate([mixed[i] for i in range(RC)], 1), cond_rows], 0)
        hi, lo = split(feat)
        feats[s, c] = jnp.concatenate([hi, lo], 0)
        h, d = activate(dot(wi_s[...], jnp.concatenate([hi, lo, hi], 0)))
        d1[s, c] = d
        both = jnp.concatenate(split(h), 0)
        h1[s, c] = both
        h, d = activate(dot_stacked(wm_s[...], both))
        d2[s, c] = d
        both = jnp.concatenate(split(h), 0)
        h2[s, c] = both
        raw = dot_stacked(wo_s[...], both)
        x = jnp.stack([raw[:4, i * C:(i + 1) * C] for i in range(RC)], 0)
        e = jnp.exp(-jnp.abs(x))
        r = 1.0 / (1.0 + e)
        sg = jnp.where(x >= 0, r, e * r)
        log1p = jnp.where(
            e < 0.0625, e * (1.0 - e * (1 / 2 - e * (1 / 3 - e * (1 / 4 - e * (1 / 5 - e * (1 / 6)))))), jnp.log(1.0 + e)
        )
        sp = jnp.maximum(x, 0.0) + log1p
        gate[s, pl.ds(c * RC, RC)] = sg
        emit[s, pl.ds(c * RC, RC)] = jnp.where(chan == 0, STEP_DEPTH * sp, sg)

    def marched(ref, rows, m):
        return jnp.where(back, ref[S - 1 - m, rows], ref[m, rows])

    def part_copy(c, k, brick):
        rows = pl.ds(c * RC, RC)
        return pltpu.make_async_remote_copy(
            src_ref=part.at[brick, rows], dst_ref=part.at[brick, rows],
            send_sem=part_send.at[c, k], recv_sem=part_recv.at[c, k],
            device_id=(v, (b + k) % bricks), device_id_type=MESH,
        )

    def composite(c):
        rows = pl.ds(c * RC, RC)
        transmit = jnp.ones((RC, 1, C), F32)
        colour = jnp.zeros((RC, 4, C), F32)
        for m in range(S):
            em = marched(emit, rows, m)
            opacity, e = one_minus_exp(em[:, 0:1, :])
            colour = colour + (transmit * opacity) * em
            transmit = transmit * e
        part[b, rows] = jnp.where(chan == 0, transmit, colour)

    def cot_copy(k, brick):
        rows = pl.ds(brick * RB, RB)
        return pltpu.make_async_remote_copy(
            src_ref=cots.at[rows], dst_ref=cots.at[rows],
            send_sem=cot_send.at[k], recv_sem=cot_recv.at[k],
            device_id=(v, (b + k) % bricks), device_id_type=MESH,
        )

    def halo_copy():
        return pltpu.make_async_remote_copy(
            src_ref=vol.at[0], dst_ref=halo, send_sem=halo_sems.at[0], recv_sem=halo_sems.at[1],
            device_id=(v, (b + bricks - 1) % bricks), device_id_type=MESH,
        )

    for s in range(S - 1):
        resample(s)

    ahead = nch // 2
    for s in range(S - 1):
        @pl.loop(0, ahead)
        def _(c, s=s):
            forward(s, c)

    pl.semaphore_wait(barrier, N - 1)

    @pl.when(b > 0)
    def _():
        halo_copy().start()

    for k in range(1, bricks):
        cot_copy(k, b).start()

    for s in range(S - 1):
        @pl.loop(ahead, nch)
        def _(c, s=s):
            forward(s, c)

    @pl.when(b == bricks - 1)
    def _():
        halo[...] = jnp.zeros_like(halo)

    @pl.when(b < bricks - 1)
    def _():
        halo_copy().wait_recv()

    resample(S - 1)

    @pl.loop(0, nch)
    def _(c):
        forward(S - 1, c)
        composite(c)
        for k in range(1, bricks):
            part_copy(c, k, b).start()

    for k in range(1, bricks):
        cot_copy(k, (b + bricks - k) % bricks).wait_recv()
    grads[...] = jnp.zeros_like(grads)
    sum_in[...] = jnp.zeros_like(sum_in)
    sum_out[...] = jnp.zeros_like(sum_out)
    position = jnp.where(back, bricks - 1 - b, b)

    def ordered(rows, p):
        return jnp.where(back, part[bricks - 1 - p, rows], part[p, rows])

    @pl.loop(0, nch)
    def _(c):
        rows = pl.ds(c * RC, RC)
        for k in range(1, bricks):
            part_copy(c, k, (b + bricks - k) % bricks).wait_recv()
        front = jnp.ones((RC, 1, C), F32)
        behind = jnp.zeros((RC, 4, C), F32)
        for p in range(bricks - 1):
            front = jnp.where(p < position, front * ordered(rows, p)[:, 0:1, :], front)
        for p in reversed(range(1, bricks)):
            here = ordered(rows, p)
            behind = jnp.where(p > position, here + here[:, 0:1, :] * behind, behind)
        grad = cots[rows] * front
        behind = jnp.sum(jnp.where(chan == 0, 0.0, grad * behind), 1, keepdims=True)
        transmit = jnp.ones((RC, 1, C), F32)
        steps = []
        for m in range(S):
            em = marched(emit, rows, m)
            opacity, e = one_minus_exp(em[:, 0:1, :])
            steps.append((em, marched(gate, rows, m), transmit * opacity, transmit * e))
            transmit = transmit * e
        tail = behind * transmit
        draws = [None] * S
        for m in reversed(range(S)):
            em, sg, weight, later = steps[m]
            q = jnp.sum(jnp.where(chan == 0, 0.0, grad * em), 1, keepdims=True)
            d_optical = q * later - tail
            tail = tail + q * weight
            draws[m] = jnp.where(chan == 0, d_optical * STEP_DEPTH * sg, grad * weight * (sg * (1.0 - sg)))
        for s in range(S):
            draw = jnp.where(back, draws[S - 1 - s], draws[s])
            draw = jnp.concatenate([draw[i] for i in range(RC)], 1)
            draw = jnp.concatenate([draw, jnp.zeros_like(draw)], 0)
            high = draw.astype(BF16).astype(F32)
            low = draw - high
            d_raw = jnp.concatenate([high, low, high, jnp.zeros_like(high)], 0).astype(BF16)
            g_out = blocks(h2[s, c], d_raw[:2 * TILE])
            du2 = dot(wob_s[...], d_raw) * d2[s, c]
            both = jnp.concatenate(split(du2), 0)
            g_mid = blocks(h1[s, c], both)
            du1 = dot_stacked(wmb_s[...], both) * d1[s, c]
            g_in = blocks(jnp.concatenate(split(du1), 0), feats[s, c])
            sum_in[...] += g_in
            grads[2:T - 1] += g_mid.reshape(T - 3, TILE, hid)
            sum_out[...] += g_out

    grads[0:2] = sum_in[...].T.reshape(2, TILE, hid)
    grads[T - 1] = sum_out[...].T

    def owner(t):
        return (t * N) // T

    def tile_copy(t, slot):
        return pltpu.make_async_remote_copy(
            src_ref=grads.at[t], dst_ref=landed.at[slot],
            send_sem=tile_send.at[t], recv_sem=tile_recv.at[slot],
            device_id=place(owner(t)), device_id_type=MESH,
        )

    def last_copy(t, k):
        return pltpu.make_async_remote_copy(
            src_ref=final.at[t], dst_ref=final.at[t],
            send_sem=last_send.at[k], recv_sem=last_recv.at[t],
            device_id=place((me + k) % N), device_id_type=MESH,
        )

    @pl.loop(0, T)
    def _(i):
        t = (i + me) % T

        @pl.when(owner(t) != me)
        def _():
            tile_copy(t, (me - owner(t) + N - 1) % N).start()

    own = pl.ds(b * RB, RB)
    transmit = jnp.ones((RB, 1, C), F32)
    colour = jnp.zeros((RB, 4, C), F32)
    for p in range(bricks):
        here = ordered(own, p)
        colour = colour + transmit * here
        transmit = transmit * here[:, 0:1, :]
    for i in range(RB):
        for c in range(3):
            image[0, c, pl.ds(i, 1), :] = colour[i, 1 + c:2 + c, :]

    my_tile = (me * T + N - 1) // N
    owns = owner(my_tile) == me

    @pl.when(owns)
    def _():
        @pl.loop(0, N - 1)
        def _(k):
            tile_copy(my_tile, k).wait_recv()

        final[my_tile] = grads[my_tile] + jnp.sum(landed[...], 0)

        @pl.loop(1, N)
        def _(k):
            last_copy(my_tile, k).start()

    @pl.when(b > 0)
    def _():
        halo_copy().wait_send()

    for k in range(1, bricks):
        cot_copy(k, b).wait_send()

    @pl.loop(0, nch)
    def _(c):
        for k in range(1, bricks):
            part_copy(c, k, b).wait_send()

    @pl.loop(0, T)
    def _(t):
        @pl.when(owner(t) != me)
        def _():
            tile_copy(t, 0).wait_send()
            last_copy(t, 1).wait_recv()

    final_out[...] = final[...]

    @pl.when(owns)
    def _():
        @pl.loop(1, N)
        def _(k):
            last_copy(my_tile, k).wait_send()


def deliver(picture, tiles, image, out_in, out_mid, out_out):
    T, _, hid = tiles.shape
    image[...] = picture[...]
    out_in[...] = tiles[0:2].reshape(2 * TILE, hid)
    out_mid[...] = tiles[2:T - 1].reshape(hid, hid)
    out_out[...] = tiles[T - 1][:4]


def per_device(volume, offsets, shifts, order, cond, w_in, w_mid, w_out, cot_image):
    views, bricks = lax.axis_size("view"), lax.axis_size("brick")
    N = views * bricks
    S, CH, R, C = volume.shape
    RB = cot_image.shape[2]
    fin, hid = w_in.shape
    RC = 16 if R % 16 == 0 else R
    nch = R // RC
    n = RC * C
    T = (fin + hid) // TILE + 1
    vmem = pl.BlockSpec(memory_space=pltpu.VMEM)
    far = pl.BlockSpec(memory_space=pltpu.HBM)
    smem = pl.BlockSpec(memory_space=pltpu.SMEM)
    kept = lambda rows, kind: pltpu.VMEM((S, nch, rows, n), kind)
    dma = lambda *shape: pltpu.SemaphoreType.DMA(shape)
    image, tiles = pl.pallas_call(
        functools.partial(kernel, views, bricks, S, R, C, RC, RB, hid),
        out_shape=(
            jax.ShapeDtypeStruct((1, 3, RB, C), F32),
            jax.ShapeDtypeStruct((T, TILE, hid), F32),
        ),
        in_specs=[far, smem, smem, smem, smem, far, far, far, far],
        out_specs=(vmem, vmem),
        scratch_shapes=[
            pltpu.VMEM((S, CH * R, C), F32),
            pltpu.VMEM(w_in.shape, F32),
            pltpu.VMEM(w_mid.shape, F32),
            pltpu.VMEM(w_out.shape[::-1], F32),
            pltpu.VMEM(cot_image.shape, F32),
            dma(5),
            pltpu.VMEM((CH * R, C), F32),
            pltpu.VMEM((S, 2 * R + 1, CH, C), F32),
            kept(2 * fin, BF16), kept(2 * hid, BF16), kept(hid, F32), kept(2 * hid, BF16), kept(hid, F32),
            pltpu.VMEM((S, R, 4, C), F32),
            pltpu.VMEM((S, R, 4, C), F32),
            pltpu.VMEM((bricks, R, 4, C), F32),
            pltpu.VMEM((R, 4, C), F32),
            pltpu.VMEM((hid, 3 * fin), BF16),
            pltpu.VMEM((2 * hid, 2 * hid), BF16),
            pltpu.VMEM((2 * TILE, 2 * hid), BF16),
            pltpu.VMEM((2 * hid, 2 * hid), BF16),
            pltpu.VMEM((hid, 4 * TILE), BF16),
            pltpu.VMEM((T, TILE, hid), F32),
            pltpu.VMEM((hid, fin), F32),
            pltpu.VMEM((hid, TILE), F32),
            pltpu.VMEM((N - 1, TILE, hid), F32),
            pltpu.VMEM((T, TILE, hid), F32),
            dma(2), dma(bricks), dma(bricks), dma(nch, bricks), dma(nch, bricks),
            dma(T), dma(N - 1), dma(N), dma(T),
        ],
        compiler_params=pltpu.CompilerParams(
            collective_id=0, has_side_effects=True, vmem_limit_bytes=60 * 1024 * 1024
        ),
        cost_estimate=pl.CostEstimate(
            flops=2 * S * R * C * hid * (3 * hid + 3 * fin + 12), bytes_accessed=4 * volume.size,
            transcendentals=2 * S * R * C * hid,
        ),
    )(volume.reshape(S, CH * R, C), offsets, shifts, order, cond, w_in, w_mid, w_out.T, cot_image)
    image, g_in, g_mid, g_out = pl.pallas_call(
        deliver,
        out_shape=(
            jax.ShapeDtypeStruct((1, 3, RB, C), F32),
            jax.ShapeDtypeStruct((fin, hid), F32),
            jax.ShapeDtypeStruct((hid, hid), F32),
            jax.ShapeDtypeStruct((4, hid), F32),
        ),
        in_specs=[vmem, vmem],
        out_specs=(vmem, vmem, vmem, vmem),
        compiler_params=pltpu.CompilerParams(vmem_limit_bytes=60 * 1024 * 1024),
    )(image, tiles)
    return image, g_in, g_mid, g_out.T


def solution(mesh):
    placed = (
        P("brick", None, None, None),
        P("view", None),
        P("view", None),
        P("view"),
        P("view", None),
        P(),
        P(),
        P(),
        P("view", None, "brick", None),
    )
    return jax.shard_map(
        per_device,
        mesh=mesh,
        in_specs=placed,
        out_specs=(P("view", None, "brick", None), P(), P(), P()),
        check_vma=False,
    )
```
